256 devices in a mesh: seq: 128 (over y, z, x_lo, core), chan: 2 (over x_hi).
Axes of the slice: x: 4 (x_hi: 2, x_lo: 2; x = x_hi * 2 + x_lo), y: 4, z: 8, core: 2. Of those that a mesh axis runs over, the one named last changes fastest.
Arguments:
- inputs: bfloat16 [262144, 256], P('seq', 'chan'), may hold values from -6 to 6
- cotangent: bfloat16 [262144, 256], P('seq', 'chan'), may hold values from -18 to 18
- residues: float32 [16, 16], replicated, may hold values from -4 to 4
- decay_rates: float32 [16, 16], replicated, may hold values from 1.9073486e-06 to 0.0333333333
- skip_weight: float32 [256], P('chan'), may hold values from -4 to 4
Outputs:
- input_grad: bfloat16 [262144, 256], P('seq', 'chan')
- residue_grad: float32 [16, 16], replicated
- skip_grad: float32 [256], P('chan')
The draws below stay inside these ranges and needn't reach their ends.
All inputs are finite; a program needn't handle non-finite values.
Results may differ from the reference program's by a relative error of at most 0.0012.
Values may be sent and summed in bfloat16 or wider, within the bound.
A program may use at most 64 MiB of HBM per device.

```python
import math
import jax
import jax.numpy as jnp
from jax import lax

CH = 256
GROUP = 16
MODES = 16
NG = 16
SEQ = 262144


def draw_decay_rates(key, part):
    key = jax.random.fold_in(key, 7)
    pick_key, slow_key, fast_key = jax.random.split(key, 3)
    slow_lower = jnp.log(0.5 / SEQ)
    slow_upper = jnp.log(2.0 / SEQ)
    fast_upper = jnp.log(1.0 / 30.0)
    slow_share = 0.5
    slow_rates = jnp.exp(jax.random.uniform(slow_key, (NG, MODES), minval=slow_lower, maxval=slow_upper))
    fast_rates = jnp.exp(jax.random.uniform(fast_key, (NG, MODES), minval=slow_upper, maxval=fast_upper))
    chooser = jax.random.uniform(pick_key, (NG, MODES))
    return jnp.where(chooser < slow_share, slow_rates, fast_rates).astype(jnp.float32)


def draw_cotangent(key, part):
    key = jax.random.fold_in(key, 11)
    position = jnp.arange(SEQ, dtype=jnp.float32)[:, None] / SEQ
    values = jnp.clip(jax.random.normal(key, (SEQ, CH)), -6.0, 6.0)
    growth = jnp.exp(position * jnp.log(3.0))
    return (values * growth).astype(jnp.bfloat16)


def block_levels(own_key, extent, shards, least, high):
    loudness = 1.0
    for dim, parts in shards:
        heights = jax.random.uniform(jax.random.fold_in(jax.random.fold_in(own_key, 6), dim), (parts,), jnp.float32, least / len(shards), high / len(shards))
        loudness = loudness * jnp.repeat(jnp.exp(heights), extent[dim] // parts).reshape((-1,) + (1,) * (len(extent) - 1 - dim))
    return loudness


def scatter_about(key, dims, deviation, reach, shards=(), held_as=jnp.bfloat16):
    level = block_levels(key, dims, shards, -0.22, 0.18) if shards else 1.0
    entries = jax.random.normal(key, dims, jnp.float32) * deviation * level
    return jnp.minimum(jnp.maximum(entries, -reach), reach).astype(held_as)


def setup_inputs(seed: int = 0) -> dict:
    splits = jax.random.split(jax.random.key(seed), 6)
    inputs = scatter_about(splits[0], (SEQ, CH), 1.0, 6.0, ((0, 128), (1, 2)))
    cotangent = draw_cotangent(jax.random.fold_in(splits[5], 71), 0)
    residues = scatter_about(splits[2], (NG, MODES), 1.0, 4.0, (), jnp.float32)
    decay_rates = draw_decay_rates(jax.random.fold_in(splits[5], 71), 0)
    skip_weight = scatter_about(splits[4], (CH,), 1.0, 4.0, ((0, 2),), jnp.float32)
    return dict(inputs=inputs, cotangent=cotangent, residues=residues, decay_rates=decay_rates, skip_weight=skip_weight)


def reference(inputs, cotangent, residues, decay_rates, skip_weight):
    length = inputs.shape[0]
    mode_norm = jnp.sqrt(-jnp.expm1(-2.0 * decay_rates))
    mode_coefs = residues * mode_norm
    x_groups = jnp.transpose(inputs.reshape(length, GROUP, NG), (2, 1, 0))
    y_groups = jnp.transpose(cotangent.reshape(length, GROUP, NG), (2, 1, 0))
    offsets = jnp.arange(length, dtype=jnp.float32)
    padded_len = 2 * length

    def per_filter(packed):
        x_rows, y_rows, rate_row, coef_row = packed
        powers = jnp.exp(-offsets[:, None] * rate_row[None, :])
        filter_taps = jnp.dot(powers, coef_row, precision=lax.Precision.HIGHEST)
        taps_freq = jnp.fft.rfft(filter_taps, n=padded_len)
        y_freq = jnp.fft.rfft(y_rows.astype(jnp.float32), n=padded_len, axis=-1)
        x_freq = jnp.fft.rfft(x_rows.astype(jnp.float32), n=padded_len, axis=-1)
        dx_rows = jnp.fft.irfft(y_freq * jnp.conj(taps_freq)[None, :], n=padded_len, axis=-1)[:, :length]
        lag_sums = jnp.fft.irfft(lax.optimization_barrier(jnp.sum(jnp.conj(x_freq) * y_freq, axis=0)), n=padded_len)[:length]
        grad_row = jnp.dot(lag_sums, powers, precision=lax.Precision.HIGHEST)
        return (dx_rows, grad_row)
    dx_groups, grads = lax.map(per_filter, (x_groups, y_groups, decay_rates, mode_coefs))
    correlation = jnp.transpose(dx_groups, (2, 1, 0)).reshape(length, CH)
    input_grad = (correlation + skip_weight[None, :] * cotangent.astype(jnp.float32)).astype(jnp.bfloat16)
    residue_grad = grads * mode_norm / math.sqrt(GROUP * length)
    skip_grad = lax.optimization_barrier(jnp.sum(inputs.astype(jnp.float32) * cotangent.astype(jnp.float32), axis=0)) / math.sqrt(length)
    return (input_grad, residue_grad, skip_grad)
```

```python
import math

import jax
import jax.numpy as jnp
from jax import lax
from jax.experimental import pallas as pl
from jax.experimental.pallas import tpu as pltpu
from jax.sharding import PartitionSpec as P

MESH = pl.DeviceIdType.MESH
F32 = jnp.float32
BF16 = jnp.bfloat16
NG = 16
MODES = 16
GROUP = 16
TOK = 2048
CD = 128
BL = 128
NB = TOK // BL
NQ, NZ, NY = 4, 8, 4


def split(v):
    hi = v.astype(BF16)
    return hi, (v - hi.astype(F32)).astype(BF16)


def nn(a, b):
    return lax.dot_general(a, b, (((1,), (0,)), ((), ())), preferred_element_type=F32)


def nt(a, b):
    return lax.dot_general(a, b, (((1,), (1,)), ((), ())), preferred_element_type=F32)


def iota(shape, dim):
    return lax.broadcasted_iota(jnp.int32, shape, dim)


def fold(h):
    h = h + pltpu.roll(h, 64, 1)
    h = h + pltpu.roll(h, 32, 1)
    return h + pltpu.roll(h, 16, 1)


def pack(h):
    h = fold(h)
    keep = iota((8, CD), 1) // 16 == iota((8, CD), 0)
    first = jnp.sum(jnp.where(keep, h[:8], 0.0), axis=0, keepdims=True)
    second = jnp.sum(jnp.where(keep, h[8:], 0.0), axis=0, keepdims=True)
    row = iota((8, CD), 0)
    return jnp.where(row == 0, first, jnp.where(row == 1, second, 0.0))


def unpack(tile):
    keep = iota((8, CD), 1) // 16 == iota((8, CD), 0)
    return jnp.concatenate(
        [jnp.where(keep, tile[0:1], 0.0), jnp.where(keep, tile[1:2], 0.0)], axis=0
    )


def extract(full):
    group_of = iota((MODES, CD), 1) % NG
    out = jnp.zeros((MODES, CD), F32)
    for g in range(NG):
        out = out + jnp.where(group_of == g, full[MODES * g : MODES * (g + 1)], 0.0)
    return out


def suffix(load_s, count, w):
    acc = load_s(count - 1)
    for i in range(count - 2, -1, -1):
        acc = load_s(i) + w * acc
    return acc


def pairs(load_s, load_t, count, w):
    acc = load_t(0)
    total = None
    for i in range(1, count):
        term = acc * load_s(i)
        total = term if total is None else total + term
        acc = load_t(i) + w * acc
    return total, acc


def kernel(
    x_hbm, y_hbm, res_ref, dec_ref, skip_ref,
    dx_hbm, rg_ref, sg_ref,
    x, y, xg, yg, tmp, rmc_ref, cmc_ref, pw, pt, after, grow, ot, loc, qh, ql, outb, rowr,
    s1, t1, g1, s2, t2, g2, s3, m3,
    load_sem, out_sem, send_sem, recv_sem,
):
    me = lax.axis_index("seq")
    half = lax.axis_index("chan")
    q = lax.rem(me, NQ)
    z = lax.rem(me // NQ, NZ)
    yy = me // (NQ * NZ)

    def at(y_i, z_i, q_i, h_i):
        return {"seq": (y_i * NZ + z_i) * NQ + q_i, "chan": h_i}

    quad_peers = [at(yy, z, lax.rem(q + NQ - k, NQ), half) for k in range(1, NQ)]
    z_peers = [at(yy, lax.rem(z + NZ - k, NZ), q, half) for k in range(1, NZ)]
    y_peers = [at(lax.rem(yy + NY - k, NY), z, q, half) for k in range(1, NY)]
    o_peers = [at(lax.rem(yy + NY - k, NY), z, q, 1 - half) for k in range(NY)]

    load_y = pltpu.make_async_copy(y_hbm, y, load_sem.at[0])
    load_x = pltpu.make_async_copy(x_hbm, x, load_sem.at[1])
    load_y.start()
    load_x.start()
    barrier = pltpu.get_barrier_semaphore()
    everyone = quad_peers + z_peers + y_peers + o_peers
    for peer in everyone:
        pl.semaphore_signal(barrier, inc=1, device_id=peer, device_id_type=MESH)

    sent = []

    def send(buf, peers, first_slot, sem):
        copies = []
        for k, peer in enumerate(peers):
            slot = first_slot + k
            copy = pltpu.make_async_remote_copy(
                src_ref=buf.at[0],
                dst_ref=buf.at[slot],
                send_sem=send_sem.at[sem + k],
                recv_sem=recv_sem.at[sem + k],
                device_id=peer,
                device_id_type=MESH,
            )
            copy.start()
            copies.append(copy)
        sent.extend(copies)
        return copies

    def arrive(copies):
        for copy in copies:
            copy.wait_recv()

    rates = dec_ref[...]
    tmp[...] = jnp.zeros_like(tmp)
    for k in range(CD // NG):
        tmp[NG * k : NG * (k + 1), 0:MODES] = rates
    rmc = jnp.transpose(tmp[...])[:MODES]
    rmc_ref[...] = rmc
    span = 2 * BL
    ahead = iota((MODES, span), 1).astype(F32)
    behind = span - ahead
    for g in range(NG):
        column = jnp.broadcast_to(rmc[:, g : g + 1], (MODES, span))
        pw[MODES * g : MODES * (g + 1), :] = jnp.exp(-(column * ahead))
        pt[MODES * g : MODES * (g + 1), :] = jnp.exp(-(column * behind))

    step = pt[:, 0:1]
    wide = jnp.broadcast_to(step, (NG * MODES, 2 * CD))
    half_decay = jnp.exp(-(float(TOK // 2) * rmc))
    blocks = TOK // 2 // span

    def summary(ref, powers, order):
        hi, lo = split(powers[...])
        total = None
        for b in order:
            both = jnp.concatenate(
                [ref[b * span : (b + 1) * span, :], ref[TOK // 2 + b * span : TOK // 2 + (b + 1) * span, :]],
                axis=1,
            )
            part = nn(hi, both) + nn(lo, both)
            total = part if total is None else part + wide * total
        return extract(total[:, :CD]), extract(total[:, CD:])

    load_y.wait()
    first, second = summary(y, pw, range(blocks - 1, -1, -1))
    s1[0] = first + half_decay * second
    load_x.wait()
    first, second = summary(x, pt, range(blocks))
    t1[0] = second + half_decay * first

    pl.semaphore_wait(barrier, len(everyone))
    c_s1 = send(s1, quad_peers, 1, 0)
    c_t1 = send(t1, quad_peers, 1, 3)

    row_c, lane_c = iota((CD, CD), 0), iota((CD, CD), 1)
    perm = jnp.where(lane_c == (row_c % 8) * NG + row_c // 8, 1.0, 0.0).astype(BF16)
    flip = jnp.where(lane_c + row_c == BL - 1, 1.0, 0.0).astype(BF16)

    def regroup(k, skip_sum):
        rows = pl.ds(pl.multiple_of(k * span, span), span)
        xb, yb = x[rows, :], y[rows, :]
        for src, dst in ((xb, xg), (yb, yg)):
            turned = nt(perm, src)
            for g in range(NG):
                piece = turned[8 * g : 8 * (g + 1)]
                dst[g, pl.ds(pl.multiple_of(k * 16, 16), 16), :] = jnp.concatenate(
                    [piece[:, :BL], piece[:, BL:]], axis=0
                ).astype(BF16)
        return skip_sum + jnp.sum(xb.astype(F32) * yb.astype(F32), axis=0, keepdims=True)

    skip_sum = lax.fori_loop(0, NB // 2, regroup, jnp.zeros((1, CD), F32))

    def gram_one(g, h):
        gs = pl.ds(pl.multiple_of(g * MODES, MODES), MODES)
        xq, yq = xg[g], yg[g]
        turned = nt(flip, xq).astype(BF16)
        gram = nn(turned, yq)
        gram = pltpu.roll(gram, 1, 1, stride=1, stride_axis=0)
        lag = jnp.sum(jnp.where(lane_c <= row_c, gram, 0.0), axis=0, keepdims=True)
        powers = pw[gs, :][:, :BL]
        tails = pt[gs, :][:, BL:]
        column = jnp.sum(powers * lag, axis=1, keepdims=True)
        ph, pl_ = split(powers)
        th, tl = split(tails)
        states = nt(yq, ph) + nt(yq, pl_)
        ends = nt(xq, th) + nt(xq, tl)
        decay = jnp.exp(-(float(BL) * dec_ref[pl.ds(g, 1), :]))
        acc = jnp.zeros((8, MODES), F32)
        pieces = [acc]
        for b in range(NB - 1, 0, -1):
            acc = states[8 * b : 8 * (b + 1)] + decay * acc
            pieces.append(acc)
        held = jnp.concatenate(pieces[::-1], axis=0)
        after[g] = held
        grow[pl.ds(g, 1), 0:MODES] = jnp.sum(ends * held, axis=0, keepdims=True)
        return h + jnp.where(iota((MODES, CD), 1) == g, column, 0.0)

    def gram_some(i, h):
        for j in range(4):
            h = gram_one(i * 4 + j, h)
        return h

    h = jnp.zeros((MODES, CD), F32)
    h = lax.fori_loop(0, 2, gram_some, h)

    dev = jnp.exp(-(float(TOK) * rmc))
    quad = jnp.exp(-(float(TOK * NQ) * rmc))
    slab = jnp.exp(-(float(TOK * NQ * NZ) * rmc))
    arrive(c_s1)
    s2[0] = suffix(lambda i: s1[lax.rem(i - q + NQ, NQ)], NQ, dev)
    c_s2 = send(s2, z_peers, 1, 6)
    arrive(c_t1)
    load_s1 = lambda i: s1[lax.rem(i - q + NQ, NQ)]
    p1, tq = pairs(load_s1, lambda i: t1[lax.rem(i - q + NQ, NQ)], NQ, dev)
    t2[0] = tq
    c_t2 = send(t2, z_peers, 1, 13)

    h = lax.fori_loop(2, 4, gram_some, h)
    tmp[...] = jnp.zeros_like(tmp)
    tmp[0:NG, 0:MODES] = grow[:, 0:MODES]
    h = h + jnp.transpose(tmp[...])[:MODES]
    g1[0] = pack(h) + jnp.where(iota((8, CD), 0) == 2, skip_sum, 0.0)
    c_g1 = send(g1, quad_peers, 1, 20)

    twice = 2.0 * rates
    series = twice * (1.0 - twice / 2 * (1.0 - twice / 3 * (1.0 - twice / 4 * (
        1.0 - twice / 5 * (1.0 - twice / 6 * (1.0 - twice / 7 * (1.0 - twice / 8)))))))
    norm = jnp.sqrt(jnp.where(twice < 0.25, series, 1.0 - jnp.exp(-twice)))
    coef = res_ref[...] * norm
    tmp[...] = jnp.zeros_like(tmp)
    for k in range(CD // NG):
        tmp[NG * k : NG * (k + 1), 0:MODES] = coef
    cmc_ref[...] = jnp.transpose(tmp[...])[:MODES]

    def local_one(g):
        gs = pl.ds(pl.multiple_of(g * MODES, MODES), MODES)
        yq = yg[g]
        pick = iota((MODES, CD), 1) == g
        column = jnp.sum(jnp.where(pick, cmc_ref[...], 0.0), axis=1, keepdims=True)
        reach = column * pt[gs, :][:, BL:]
        lane = iota((MODES, BL), 1)
        taps = jnp.sum(jnp.where(lane == 0, column, reach), axis=0, keepdims=True)
        toep = pltpu.roll(jnp.broadcast_to(taps, (BL, BL)), 0, 1, stride=1, stride_axis=0)
        th, tl = split(jnp.where(lane_c <= row_c, toep, 0.0))
        ah, al = split(after[g])
        wh, wl = split(reach)
        out = nn(yq, th) + nn(yq, tl) + (nn(ah, wh) + nn(al, wh) + nn(ah, wl))
        for b in range(NB):
            ot[b, pl.ds(g, 8, stride=NG), :] = out[8 * b : 8 * (b + 1)]

    def local_some(i, _):
        for j in range(4):
            local_one(i * 4 + j)
        return _

    lax.fori_loop(0, 2, local_some, 0)
    arrive(c_g1)
    g2[0] = g1[0] + g1[1] + g1[2] + g1[3] + pack(p1)
    c_g2 = send(g2, z_peers, 1, 23)
    lax.fori_loop(2, 4, local_some, 0)

    skip_row = skip_ref[...].reshape(1, CD)

    def settle(b, _):
        rows = pl.ds(pl.multiple_of(b * BL, BL), BL)
        loc[rows, :] = jnp.transpose(ot[b]) + skip_row * y[rows, :].astype(F32)
        return _

    lax.fori_loop(0, NB, settle, 0)

    arrive(c_s2)
    load_s2 = lambda i: s2[lax.rem(i - z + NZ, NZ)]
    s3[0] = suffix(load_s2, NZ, quad)
    c_s3 = send(s3, y_peers, 1, 30)

    column = jnp.concatenate(
        [jnp.broadcast_to(rmc[:, g : g + 1], (MODES, CD)) for g in range(NG)], axis=0
    )
    rowr[...] = jnp.transpose(column)[0:8]
    hl = TOK // 2

    def reach_some(b, _):
        rows = pl.ds(pl.multiple_of(b * BL, BL), BL)
        left = (hl - b * BL - iota((BL, NG * MODES), 0)).astype(F32)
        hi, lo = split(jnp.exp(-(left * rowr[0:1, :])))
        qh[rows, :] = hi
        ql[rows, :] = lo
        return _

    lax.fori_loop(0, hl // BL, reach_some, 0)

    arrive(c_t2)
    p2, ty = pairs(load_s2, lambda i: t2[lax.rem(i - z + NZ, NZ)], NZ, quad)
    arrive(c_g2)
    gz = g2[0]
    for k in range(1, NZ):
        gz = gz + g2[k]
    m3[0, 0:16] = s3[0]
    m3[0, 16:32] = ty
    m3[0, 32:40] = gz + pack(p2)
    c_m3 = send(m3, y_peers + o_peers, 1, 33)

    arrive(c_s3)
    one = jnp.ones((MODES, CD), F32)
    zero = jnp.zeros((MODES, CD), F32)
    inc_y, w = zero, one
    for k in range(1, NY):
        inc_y = inc_y + jnp.where(yy + k < NY, w, zero) * s3[k]
        w = w * slab
    inc_z, w = zero, one
    for k in range(1, NZ):
        inc_z = inc_z + jnp.where(z + k < NZ, w, zero) * s2[k]
        w = w * quad
    inc_q, w = zero, one
    for k in range(1, NQ):
        inc_q = inc_q + jnp.where(q + k < NQ, w, zero) * s1[k]
        w = w * dev
    to_slab = jnp.exp(-(((NZ - 1 - z) * (TOK * NQ)).astype(F32) * rmc))
    to_quad = jnp.exp(-(((NQ - 1 - q) * TOK).astype(F32) * rmc))
    inc = inc_q + to_quad * (inc_z + to_slab * inc_y)

    late = cmc_ref[...] * inc
    early = late * half_decay
    group_of = iota((MODES, CD), 1) % NG

    def spread(v):
        return jnp.concatenate([jnp.where(group_of == g, v, 0.0) for g in range(NG)], axis=0)

    def both(v, u):
        return jnp.concatenate([spread(v), spread(u)], axis=1).astype(BF16)

    eh = early.astype(BF16).astype(F32)
    lh = late.astype(BF16).astype(F32)
    a_hi = both(eh, lh)
    a_lo = both(early - eh, late - lh)

    def finish(b, _):
        rows = pl.ds(pl.multiple_of(b * BL, BL), BL)
        rows2 = pl.ds(pl.multiple_of(hl + b * BL, BL), BL)
        hi, lo = qh[rows, :], ql[rows, :]
        add = nn(hi, a_hi) + nn(hi, a_lo) + nn(lo, a_hi)
        outb[rows, :] = (loc[rows, :] + add[:, :CD]).astype(BF16)
        outb[rows2, :] = (loc[rows2, :] + add[:, CD:]).astype(BF16)
        return _

    lax.fori_loop(0, hl // BL, finish, 0)
    store = pltpu.make_async_copy(outb, dx_hbm, out_sem.at[0])
    store.start()

    arrive(c_m3)

    def load_y3(lo, base):
        return lambda i: m3[base + lax.rem(i - yy + NY, NY), lo : lo + 16]

    p3, _ = pairs(load_y3(0, 0), load_y3(16, 0), NY, slab)
    p4, _ = pairs(load_y3(0, 4), load_y3(16, 4), NY, slab)
    own = m3[0, 32:40] + m3[1, 32:40] + m3[2, 32:40] + m3[3, 32:40]
    other = m3[4, 32:40] + m3[5, 32:40] + m3[6, 32:40] + m3[7, 32:40]
    total_len = TOK * NQ * NZ * NY
    sg_ref[...] = (own[2:3] * (1.0 / math.sqrt(total_len))).reshape(CD)
    grads = fold(unpack(own + other) + p3 + p4)
    tmp[...] = jnp.zeros_like(tmp)
    tmp[0:MODES, :] = grads
    turned = jnp.transpose(tmp[...])[0:NG, 0:MODES]
    rg_ref[...] = turned * norm * (1.0 / math.sqrt(GROUP * total_len))

    for copy in sent:
        copy.wait_send()
    store.wait()


def shards(inputs, cotangent, residues, decay_rates, skip_weight):
    vmem = pl.BlockSpec(memory_space=pltpu.VMEM)
    hbm = pl.BlockSpec(memory_space=pl.ANY)
    return pl.pallas_call(
        kernel,
        out_shape=(
            jax.ShapeDtypeStruct((TOK, CD), BF16),
            jax.ShapeDtypeStruct((NG, MODES), F32),
            jax.ShapeDtypeStruct((CD,), F32),
        ),
        in_specs=[hbm, hbm, vmem, vmem, vmem],
        out_specs=(hbm, vmem, vmem),
        scratch_shapes=[
            pltpu.VMEM((TOK, CD), BF16),
            pltpu.VMEM((TOK, CD), BF16),
            pltpu.VMEM((NG, CD, BL), BF16),
            pltpu.VMEM((NG, CD, BL), BF16),
            pltpu.VMEM((CD, CD), F32),
            pltpu.VMEM((MODES, CD), F32),
            pltpu.VMEM((MODES, CD), F32),
            pltpu.VMEM((NG * MODES, 2 * BL), F32),
            pltpu.VMEM((NG * MODES, 2 * BL), F32),
            pltpu.VMEM((NG, CD, MODES), F32),
            pltpu.VMEM((NG, CD), F32),
            pltpu.VMEM((NB, CD, BL), F32),
            pltpu.VMEM((TOK, CD), F32),
            pltpu.VMEM((TOK // 2, NG * MODES), BF16),
            pltpu.VMEM((TOK // 2, NG * MODES), BF16),
            pltpu.VMEM((TOK, CD), BF16),
            pltpu.VMEM((8, NG * MODES), F32),
            pltpu.VMEM((NQ, MODES, CD), F32),
            pltpu.VMEM((NQ, MODES, CD), F32),
            pltpu.VMEM((NQ, 8, CD), F32),
            pltpu.VMEM((NZ, MODES, CD), F32),
            pltpu.VMEM((NZ, MODES, CD), F32),
            pltpu.VMEM((NZ, 8, CD), F32),
            pltpu.VMEM((NY, MODES, CD), F32),
            pltpu.VMEM((2 * NY, 40, CD), F32),
            pltpu.SemaphoreType.DMA((2,)),
            pltpu.SemaphoreType.DMA((1,)),
            pltpu.SemaphoreType.DMA((40,)),
            pltpu.SemaphoreType.DMA((40,)),
        ],
        compiler_params=pltpu.CompilerParams(
            collective_id=0, has_side_effects=True, vmem_limit_bytes=32 << 20
        ),
    )(inputs, cotangent, residues, decay_rates, skip_weight)


def solution(mesh):
    placed = (P("seq", "chan"), P("seq", "chan"), P(), P(), P("chan"))
    return jax.shard_map(
        shards,
        mesh=mesh,
        in_specs=placed,
        out_specs=(P("seq", "chan"), P(), P("chan")),
        check_vma=False,
    )
```

```python
import math

import jax
import jax.numpy as jnp
from jax import lax
from jax.experimental import pallas as pl
from jax.experimental.pallas import tpu as pltpu
from jax.sharding import PartitionSpec as P

MESH = pl.DeviceIdType.MESH
F32 = jnp.float32
BF16 = jnp.bfloat16
NG = 16
MODES = 16
GROUP = 16
TOK = 2048
CD = 128
BL = 128
NB = TOK // BL
NQ, NZ, NY = 4, 8, 4


def split(v):
    hi = v.astype(BF16)
    return hi, (v - hi.astype(F32)).astype(BF16)


def nn(a, b):
    return lax.dot_general(a, b, (((1,), (0,)), ((), ())), preferred_element_type=F32)


def nt(a, b):
    return lax.dot_general(a, b, (((1,), (1,)), ((), ())), preferred_element_type=F32)


def iota(shape, dim):
    return lax.broadcasted_iota(jnp.int32, shape, dim)


def fold(h):
    h = h + pltpu.roll(h, 64, 1)
    h = h + pltpu.roll(h, 32, 1)
    return h + pltpu.roll(h, 16, 1)


def pack(h):
    h = fold(h)
    keep = iota((8, CD), 1) // 16 == iota((8, CD), 0)
    first = jnp.sum(jnp.where(keep, h[:8], 0.0), axis=0, keepdims=True)
    second = jnp.sum(jnp.where(keep, h[8:], 0.0), axis=0, keepdims=True)
    row = iota((8, CD), 0)
    return jnp.where(row == 0, first, jnp.where(row == 1, second, 0.0))


def unpack(tile):
    keep = iota((8, CD), 1) // 16 == iota((8, CD), 0)
    return jnp.concatenate(
        [jnp.where(keep, tile[0:1], 0.0), jnp.where(keep, tile[1:2], 0.0)], axis=0
    )


def extract(full):
    group_of = iota((MODES, CD), 1) % NG
    out = jnp.zeros((MODES, CD), F32)
    for g in range(NG):
        out = out + jnp.where(group_of == g, full[MODES * g : MODES * (g + 1)], 0.0)
    return out


def suffix(load_s, count, w):
    acc = load_s(count - 1)
    for i in range(count - 2, -1, -1):
        acc = load_s(i) + w * acc
    return acc


def pairs(load_s, load_t, count, w):
    acc = load_t(0)
    total = None
    for i in range(1, count):
        term = acc * load_s(i)
        total = term if total is None else total + term
        acc = load_t(i) + w * acc
    return total, acc


def kernel(
    x_hbm, y_hbm, res_hbm, dec_hbm, skip_hbm,
    outb, rg_ref, sg_ref,
    x, y, res_ref, dec_ref, skip_ref, xg, yg, tmp, rmc_ref, cmc_ref, pw, pt, after, grow, ot, loc, qh, ql, rowr,
    s1, t1, g1, s2, t2, g2, s3, m3,
    load_sem, send_sem, recv_sem,
):
    me = lax.axis_index("seq")
    half = lax.axis_index("chan")
    q = lax.rem(me, NQ)
    z = lax.rem(me // NQ, NZ)
    yy = me // (NQ * NZ)

    def at(y_i, z_i, q_i, h_i):
        return {"seq": (y_i * NZ + z_i) * NQ + q_i, "chan": h_i}

    quad_peers = [at(yy, z, lax.rem(q + NQ - k, NQ), half) for k in range(1, NQ)]
    z_peers = [at(yy, lax.rem(z + NZ - k, NZ), q, half) for k in range(1, NZ)]
    y_peers = [at(lax.rem(yy + NY - k, NY), z, q, half) for k in range(1, NY)]
    o_peers = [at(lax.rem(yy + NY - k, NY), z, q, 1 - half) for k in range(NY)]

    load_y = pltpu.make_async_copy(y_hbm, y, load_sem.at[0])
    load_x = pltpu.make_async_copy(x_hbm, x, load_sem.at[1])
    load_r = pltpu.make_async_copy(res_hbm, res_ref, load_sem.at[2])
    load_d = pltpu.make_async_copy(dec_hbm, dec_ref, load_sem.at[3])
    load_k = pltpu.make_async_copy(skip_hbm, skip_ref, load_sem.at[4])
    for copy in (load_d, load_y, load_x, load_r, load_k):
        copy.start()
    barrier = pltpu.get_barrier_semaphore()
    everyone = quad_peers + z_peers + y_peers + o_peers
    for peer in everyone:
        pl.semaphore_signal(barrier, inc=1, device_id=peer, device_id_type=MESH)

    sent = []

    def send(buf, peers, first_slot, sem):
        copies = []
        for k, peer in enumerate(peers):
            slot = first_slot + k
            copy = pltpu.make_async_remote_copy(
                src_ref=buf.at[0],
                dst_ref=buf.at[slot],
                send_sem=send_sem.at[sem + k],
                recv_sem=recv_sem.at[sem + k],
                device_id=peer,
                device_id_type=MESH,
            )
            copy.start()
            copies.append(copy)
        sent.extend(copies)
        return copies

    def arrive(copies):
        for copy in copies:
            copy.wait_recv()

    load_d.wait()
    rates = dec_ref[...]
    tmp[...] = jnp.zeros_like(tmp)
    for k in range(CD // NG):
        tmp[NG * k : NG * (k + 1), 0:MODES] = rates
    rmc = jnp.transpose(tmp[...])[:MODES]
    rmc_ref[...] = rmc
    span = 2 * BL
    ahead = iota((MODES, span), 1).astype(F32)
    behind = span - ahead
    for g in range(NG):
        column = jnp.broadcast_to(rmc[:, g : g + 1], (MODES, span))
        pw[MODES * g : MODES * (g + 1), :] = jnp.exp(-(column * ahead))
        pt[MODES * g : MODES * (g + 1), :] = jnp.exp(-(column * behind))

    step = pt[:, 0:1]
    wide = jnp.broadcast_to(step, (NG * MODES, 2 * CD))
    half_decay = jnp.exp(-(float(TOK // 2) * rmc))
    blocks = TOK // 2 // span

    def summary(ref, powers, order):
        hi, lo = split(powers[...])
        total = None
        for b in order:
            both = jnp.concatenate(
                [ref[b * span : (b + 1) * span, :], ref[TOK // 2 + b * span : TOK // 2 + (b + 1) * span, :]],
                axis=1,
            )
            part = nn(hi, both) + nn(lo, both)
            total = part if total is None else part + wide * total
        return extract(total[:, :CD]), extract(total[:, CD:])

    load_y.wait()
    first, second = summary(y, pw, range(blocks - 1, -1, -1))
    s1[0] = first + half_decay * second
    load_x.wait()
    load_r.wait()
    load_k.wait()
    first, second = summary(x, pt, range(blocks))
    t1[0] = second + half_decay * first

    pl.semaphore_wait(barrier, len(everyone))
    c_s1 = send(s1, quad_peers, 1, 0)
    c_t1 = send(t1, quad_peers, 1, 3)

    row_c, lane_c = iota((CD, CD), 0), iota((CD, CD), 1)
    perm = jnp.where(lane_c == (row_c % 8) * NG + row_c // 8, 1.0, 0.0).astype(BF16)
    flip = jnp.where(lane_c + row_c == BL - 1, 1.0, 0.0).astype(BF16)

    def regroup(k, skip_sum):
        rows = pl.ds(pl.multiple_of(k * span, span), span)
        xb, yb = x[rows, :], y[rows, :]
        for src, dst in ((xb, xg), (yb, yg)):
            turned = nt(perm, src)
            for g in range(NG):
                piece = turned[8 * g : 8 * (g + 1)]
                dst[g, pl.ds(pl.multiple_of(k * 16, 16), 16), :] = jnp.concatenate(
                    [piece[:, :BL], piece[:, BL:]], axis=0
                ).astype(BF16)
        return skip_sum + jnp.sum(xb.astype(F32) * yb.astype(F32), axis=0, keepdims=True)

    skip_sum = lax.fori_loop(0, NB // 2, regroup, jnp.zeros((1, CD), F32))

    def gram_one(g, h):
        gs = pl.ds(pl.multiple_of(g * MODES, MODES), MODES)
        xq, yq = xg[g], yg[g]
        turned = nt(flip, xq).astype(BF16)
        gram = nn(turned, yq)
        gram = pltpu.roll(gram, 1, 1, stride=1, stride_axis=0)
        lag = jnp.sum(jnp.where(lane_c <= row_c, gram, 0.0), axis=0, keepdims=True)
        powers = pw[gs, :][:, :BL]
        tails = pt[gs, :][:, BL:]
        column = jnp.sum(powers * lag, axis=1, keepdims=True)
        ph, pl_ = split(powers)
        th, tl = split(tails)
        states = nt(yq, ph) + nt(yq, pl_)
        ends = nt(xq, th) + nt(xq, tl)
        decay = jnp.exp(-(float(BL) * dec_ref[pl.ds(g, 1), :]))
        acc = jnp.zeros((8, MODES), F32)
        pieces = [acc]
        for b in range(NB - 1, 0, -1):
            acc = states[8 * b : 8 * (b + 1)] + decay * acc
            pieces.append(acc)
        held = jnp.concatenate(pieces[::-1], axis=0)
        after[g] = held
        grow[pl.ds(g, 1), 0:MODES] = jnp.sum(ends * held, axis=0, keepdims=True)
        return h + jnp.where(iota((MODES, CD), 1) == g, column, 0.0)

    def gram_some(i, h):
        for j in range(4):
            h = gram_one(i * 4 + j, h)
        return h

    h = jnp.zeros((MODES, CD), F32)
    h = lax.fori_loop(0, 2, gram_some, h)

    dev = jnp.exp(-(float(TOK) * rmc))
    quad = jnp.exp(-(float(TOK * NQ) * rmc))
    slab = jnp.exp(-(float(TOK * NQ * NZ) * rmc))
    arrive(c_s1)
    s2[0] = suffix(lambda i: s1[lax.rem(i - q + NQ, NQ)], NQ, dev)
    c_s2 = send(s2, z_peers, 1, 6)
    arrive(c_t1)
    load_s1 = lambda i: s1[lax.rem(i - q + NQ, NQ)]
    p1, tq = pairs(load_s1, lambda i: t1[lax.rem(i - q + NQ, NQ)], NQ, dev)
    t2[0] = tq
    c_t2 = send(t2, z_peers, 1, 13)

    h = lax.fori_loop(2, 4, gram_some, h)
    tmp[...] = jnp.zeros_like(tmp)
    tmp[0:NG, 0:MODES] = grow[:, 0:MODES]
    h = h + jnp.transpose(tmp[...])[:MODES]
    g1[0] = pack(h) + jnp.where(iota((8, CD), 0) == 2, skip_sum, 0.0)
    c_g1 = send(g1, quad_peers, 1, 20)

    twice = 2.0 * rates
    series = twice * (1.0 - twice / 2 * (1.0 - twice / 3 * (1.0 - twice / 4 * (
        1.0 - twice / 5 * (1.0 - twice / 6 * (1.0 - twice / 7 * (1.0 - twice / 8)))))))
    norm = jnp.sqrt(jnp.where(twice < 0.25, series, 1.0 - jnp.exp(-twice)))
    coef = res_ref[...] * norm
    tmp[...] = jnp.zeros_like(tmp)
    for k in range(CD // NG):
        tmp[NG * k : NG * (k + 1), 0:MODES] = coef
    cmc_ref[...] = jnp.transpose(tmp[...])[:MODES]

    def local_one(g):
        gs = pl.ds(pl.multiple_of(g * MODES, MODES), MODES)
        yq = yg[g]
        pick = iota((MODES, CD), 1) == g
        column = jnp.sum(jnp.where(pick, cmc_ref[...], 0.0), axis=1, keepdims=True)
        reach = column * pt[gs, :][:, BL:]
        lane = iota((MODES, BL), 1)
        taps = jnp.sum(jnp.where(lane == 0, column, reach), axis=0, keepdims=True)
        toep = pltpu.roll(jnp.broadcast_to(taps, (BL, BL)), 0, 1, stride=1, stride_axis=0)
        th, tl = split(jnp.where(lane_c <= row_c, toep, 0.0))
        ah, al = split(after[g])
        wh, wl = split(reach)
        out = nn(yq, th) + nn(yq, tl) + (nn(ah, wh) + nn(al, wh) + nn(ah, wl))
        for b in range(NB):
            ot[b, pl.ds(g, 8, stride=NG), :] = out[8 * b : 8 * (b + 1)]

    def local_some(i, _):
        for j in range(4):
            local_one(i * 4 + j)
        return _

    lax.fori_loop(0, 2, local_some, 0)
    arrive(c_g1)
    g2[0] = g1[0] + g1[1] + g1[2] + g1[3] + pack(p1)
    c_g2 = send(g2, z_peers, 1, 23)
    lax.fori_loop(2, 4, local_some, 0)

    skip_row = skip_ref[...].reshape(1, CD)

    def settle(b, _):
        rows = pl.ds(pl.multiple_of(b * BL, BL), BL)
        loc[rows, :] = jnp.transpose(ot[b]) + skip_row * y[rows, :].astype(F32)
        return _

    lax.fori_loop(0, NB, settle, 0)

    arrive(c_s2)
    load_s2 = lambda i: s2[lax.rem(i - z + NZ, NZ)]
    s3[0] = suffix(load_s2, NZ, quad)
    c_s3 = send(s3, y_peers, 1, 30)

    column = jnp.concatenate(
        [jnp.broadcast_to(rmc[:, g : g + 1], (MODES, CD)) for g in range(NG)], axis=0
    )
    rowr[...] = jnp.transpose(column)[0:8]
    hl = TOK // 2

    def reach_some(b, _):
        rows = pl.ds(pl.multiple_of(b * BL, BL), BL)
        left = (hl - b * BL - iota((BL, NG * MODES), 0)).astype(F32)
        hi, lo = split(jnp.exp(-(left * rowr[0:1, :])))
        qh[rows, :] = hi
        ql[rows, :] = lo
        return _

    lax.fori_loop(0, hl // BL, reach_some, 0)

    arrive(c_t2)
    p2, ty = pairs(load_s2, lambda i: t2[lax.rem(i - z + NZ, NZ)], NZ, quad)
    arrive(c_g2)
    gz = g2[0]
    for k in range(1, NZ):
        gz = gz + g2[k]
    m3[0, 0:16] = s3[0]
    m3[0, 16:32] = ty
    m3[0, 32:40] = gz + pack(p2)
    c_m3 = send(m3, y_peers + o_peers, 1, 33)

    arrive(c_s3)
    one = jnp.ones((MODES, CD), F32)
    zero = jnp.zeros((MODES, CD), F32)
    inc_y, w = zero, one
    for k in range(1, NY):
        inc_y = inc_y + jnp.where(yy + k < NY, w, zero) * s3[k]
        w = w * slab
    inc_z, w = zero, one
    for k in range(1, NZ):
        inc_z = inc_z + jnp.where(z + k < NZ, w, zero) * s2[k]
        w = w * quad
    inc_q, w = zero, one
    for k in range(1, NQ):
        inc_q = inc_q + jnp.where(q + k < NQ, w, zero) * s1[k]
        w = w * dev
    to_slab = jnp.exp(-(((NZ - 1 - z) * (TOK * NQ)).astype(F32) * rmc))
    to_quad = jnp.exp(-(((NQ - 1 - q) * TOK).astype(F32) * rmc))
    inc = inc_q + to_quad * (inc_z + to_slab * inc_y)

    late = cmc_ref[...] * inc
    early = late * half_decay
    group_of = iota((MODES, CD), 1) % NG

    def spread(v):
        return jnp.concatenate([jnp.where(group_of == g, v, 0.0) for g in range(NG)], axis=0)

    def both(v, u):
        return jnp.concatenate([spread(v), spread(u)], axis=1).astype(BF16)

    eh = early.astype(BF16).astype(F32)
    lh = late.astype(BF16).astype(F32)
    a_hi = both(eh, lh)
    a_lo = both(early - eh, late - lh)

    def finish(b, _):
        rows = pl.ds(pl.multiple_of(b * BL, BL), BL)
        rows2 = pl.ds(pl.multiple_of(hl + b * BL, BL), BL)
        hi, lo = qh[rows, :], ql[rows, :]
        add = nn(hi, a_hi) + nn(hi, a_lo) + nn(lo, a_hi)
        outb[rows, :] = (loc[rows, :] + add[:, :CD]).astype(BF16)
        outb[rows2, :] = (loc[rows2, :] + add[:, CD:]).astype(BF16)
        return _

    lax.fori_loop(0, hl // BL, finish, 0)

    arrive(c_m3)

    def load_y3(lo, base):
        return lambda i: m3[base + lax.rem(i - yy + NY, NY), lo : lo + 16]

    p3, _ = pairs(load_y3(0, 0), load_y3(16, 0), NY, slab)
    p4, _ = pairs(load_y3(0, 4), load_y3(16, 4), NY, slab)
    own = m3[0, 32:40] + m3[1, 32:40] + m3[2, 32:40] + m3[3, 32:40]
    other = m3[4, 32:40] + m3[5, 32:40] + m3[6, 32:40] + m3[7, 32:40]
    total_len = TOK * NQ * NZ * NY
    sg_ref[...] = (own[2:3] * (1.0 / math.sqrt(total_len))).reshape(CD)
    grads = fold(unpack(own + other) + p3 + p4)
    tmp[...] = jnp.zeros_like(tmp)
    tmp[0:MODES, :] = grads
    turned = jnp.transpose(tmp[...])[0:NG, 0:MODES]
    rg_ref[...] = turned * norm * (1.0 / math.sqrt(GROUP * total_len))

    for copy in sent:
        copy.wait_send()


def deliver(a, b, c, to_a, to_b, to_c, sems):
    copies = [
        pltpu.make_async_copy(src, dst, sems.at[i])
        for i, (src, dst) in enumerate(((a, to_a), (b, to_b), (c, to_c)))
    ]
    for copy in copies:
        copy.start()
    for copy in copies:
        copy.wait()


def shards(inputs, cotangent, residues, decay_rates, skip_weight):
    vmem = pl.BlockSpec(memory_space=pltpu.VMEM)
    hbm = pl.BlockSpec(memory_space=pltpu.HBM)
    near = pl.pallas_call(
        kernel,
        out_shape=(
            pltpu.VMEM((TOK, CD), BF16),
            pltpu.VMEM((NG, MODES), F32),
            pltpu.VMEM((CD,), F32),
        ),
        in_specs=[hbm] * 5,
        out_specs=(vmem, vmem, vmem),
        scratch_shapes=[
            pltpu.VMEM((TOK, CD), BF16),
            pltpu.VMEM((TOK, CD), BF16),
            pltpu.VMEM((NG, MODES), F32),
            pltpu.VMEM((NG, MODES), F32),
            pltpu.VMEM((CD,), F32),
            pltpu.VMEM((NG, CD, BL), BF16),
            pltpu.VMEM((NG, CD, BL), BF16),
            pltpu.VMEM((CD, CD), F32),
            pltpu.VMEM((MODES, CD), F32),
            pltpu.VMEM((MODES, CD), F32),
            pltpu.VMEM((NG * MODES, 2 * BL), F32),
            pltpu.VMEM((NG * MODES, 2 * BL), F32),
            pltpu.VMEM((NG, CD, MODES), F32),
            pltpu.VMEM((NG, CD), F32),
            pltpu.VMEM((NB, CD, BL), F32),
            pltpu.VMEM((TOK, CD), F32),
            pltpu.VMEM((TOK // 2, NG * MODES), BF16),
            pltpu.VMEM((TOK // 2, NG * MODES), BF16),
            pltpu.VMEM((8, NG * MODES), F32),
            pltpu.VMEM((NQ, MODES, CD), F32),
            pltpu.VMEM((NQ, MODES, CD), F32),
            pltpu.VMEM((NQ, 8, CD), F32),
            pltpu.VMEM((NZ, MODES, CD), F32),
            pltpu.VMEM((NZ, MODES, CD), F32),
            pltpu.VMEM((NZ, 8, CD), F32),
            pltpu.VMEM((NY, MODES, CD), F32),
            pltpu.VMEM((2 * NY, 40, CD), F32),
            pltpu.SemaphoreType.DMA((5,)),
            pltpu.SemaphoreType.DMA((40,)),
            pltpu.SemaphoreType.DMA((40,)),
        ],
        compiler_params=pltpu.CompilerParams(
            collective_id=0, has_side_effects=True, vmem_limit_bytes=32 << 20
        ),
    )(*[pltpu.with_memory_space_constraint(v, pltpu.HBM) for v in (inputs, cotangent, residues, decay_rates, skip_weight)])
    return pl.pallas_call(
        deliver,
        out_shape=(
            jax.ShapeDtypeStruct((TOK, CD), BF16),
            jax.ShapeDtypeStruct((NG, MODES), F32),
            jax.ShapeDtypeStruct((CD,), F32),
        ),
        in_specs=[vmem, vmem, vmem],
        out_specs=(hbm, hbm, hbm),
        scratch_shapes=[pltpu.SemaphoreType.DMA((3,))],
    )(*[pltpu.with_memory_space_constraint(v, pltpu.VMEM) for v in near])


def solution(mesh):
    placed = (P("seq", "chan"), P("seq", "chan"), P(), P(), P("chan"))
    return jax.shard_map(
        shards,
        mesh=mesh,
        in_specs=placed,
        out_specs=(P("seq", "chan"), P(), P("chan")),
        check_vma=False,
    )
```

```python
import math

import jax
import jax.numpy as jnp
from jax import lax
from jax.experimental import pallas as pl
from jax.experimental.pallas import tpu as pltpu
from jax.sharding import PartitionSpec as P

MESH = pl.DeviceIdType.MESH
F32 = jnp.float32
BF16 = jnp.bfloat16
NG = 16
MODES = 16
GROUP = 16
TOK = 2048
CD = 128
BL = 128
NB = TOK // BL
NQ, NZ, NY = 4, 8, 4


def split(v):
    hi = v.astype(BF16)
    return hi, (v - hi.astype(F32)).astype(BF16)


def nn(a, b):
    return lax.dot_general(a, b, (((1,), (0,)), ((), ())), preferred_element_type=F32)


def nt(a, b):
    return lax.dot_general(a, b, (((1,), (1,)), ((), ())), preferred_element_type=F32)


def iota(shape, dim):
    return lax.broadcasted_iota(jnp.int32, shape, dim)


def fold(h):
    h = h + pltpu.roll(h, 64, 1)
    h = h + pltpu.roll(h, 32, 1)
    return h + pltpu.roll(h, 16, 1)


def pack(h):
    h = fold(h)
    keep = iota((8, CD), 1) // 16 == iota((8, CD), 0)
    first = jnp.sum(jnp.where(keep, h[:8], 0.0), axis=0, keepdims=True)
    second = jnp.sum(jnp.where(keep, h[8:], 0.0), axis=0, keepdims=True)
    row = iota((8, CD), 0)
    return jnp.where(row == 0, first, jnp.where(row == 1, second, 0.0))


def unpack(tile):
    keep = iota((8, CD), 1) // 16 == iota((8, CD), 0)
    return jnp.concatenate(
        [jnp.where(keep, tile[0:1], 0.0), jnp.where(keep, tile[1:2], 0.0)], axis=0
    )


def extract(full):
    group_of = iota((MODES, CD), 1) % NG
    out = jnp.zeros((MODES, CD), F32)
    for g in range(NG):
        out = out + jnp.where(group_of == g, full[MODES * g : MODES * (g + 1)], 0.0)
    return out


def suffix(load_s, count, w):
    acc = load_s(count - 1)
    for i in range(count - 2, -1, -1):
        acc = load_s(i) + w * acc
    return acc


def pairs(load_s, load_t, count, w):
    acc = load_t(0)
    total = None
    for i in range(1, count):
        term = acc * load_s(i)
        total = term if total is None else total + term
        acc = load_t(i) + w * acc
    return total, acc


def exchange(blocks):
    bit_of = iota(blocks[0].shape, 1)
    for k in (1, 2, 4, 8):
        keep = (bit_of & k) == 0
        for i in range(NG):
            if not i & k:
                low, high = blocks[i], blocks[i | k]
                blocks[i] = jnp.where(keep, low, pltpu.roll(high, k, 1))
                blocks[i | k] = jnp.where(keep, pltpu.roll(low, CD - k, 1), high)
    return blocks


def kernel(
    x_hbm, y_hbm, res_hbm, dec_hbm, skip_hbm,
    outb, rg_ref, sg_ref,
    x, y, res_ref, dec_ref, skip_ref, xn, yn, tmp, cmc_ref, rates3, pw, pt, zs, tb, lags, after, on, loc, qh, ql,
    s1, t1, s2, t2, s3, m3, gz, gy, gq,
    load_sem, send_sem, recv_sem,
):
    me = lax.axis_index("seq")
    half = lax.axis_index("chan")
    q = lax.rem(me, NQ)
    z = lax.rem(me // NQ, NZ)
    yy = me // (NQ * NZ)

    def at(y_i, z_i, q_i, h_i):
        return {"seq": (y_i * NZ + z_i) * NQ + q_i, "chan": h_i}

    quad_peers = [(k, at(yy, z, lax.rem(q + NQ - k, NQ), half)) for k in (2, 3, 1)]
    z_peers = [(k, at(yy, lax.rem(z + NZ - k, NZ), q, half)) for k in (4, 3, 5, 2, 6, 1, 7)]
    y_peers = [(k, at(lax.rem(yy + NY - k, NY), z, q, half)) for k in (2, 1, 3)]
    o_peers = [(NY + k, at(lax.rem(yy + NY - k, NY), z, q, 1 - half)) for k in (2, 1, 3, 0)]

    load_y = pltpu.make_async_copy(y_hbm, y, load_sem.at[0])
    load_x = pltpu.make_async_copy(x_hbm, x, load_sem.at[1])
    load_r = pltpu.make_async_copy(res_hbm, res_ref, load_sem.at[2])
    load_d = pltpu.make_async_copy(dec_hbm, dec_ref, load_sem.at[3])
    load_k = pltpu.make_async_copy(skip_hbm, skip_ref, load_sem.at[4])
    load_d.start()
    load_y.start()
    barrier = pltpu.get_barrier_semaphore()
    everyone = z_peers + o_peers + y_peers + quad_peers
    for _, peer in everyone:
        pl.semaphore_signal(barrier, inc=1, device_id=peer, device_id_type=MESH)
    load_x.start()
    load_r.start()
    load_k.start()

    sent = []

    def send(buf, peers, sem):
        copies = []
        for slot, peer in peers:
            copy = pltpu.make_async_remote_copy(
                src_ref=buf.at[0],
                dst_ref=buf.at[slot],
                send_sem=send_sem.at[sem + slot],
                recv_sem=recv_sem.at[sem + slot],
                device_id=peer,
                device_id_type=MESH,
            )
            copy.start()
            copies.append(copy)
        sent.extend(copies)
        return copies

    def arrive(copies):
        for copy in copies:
            copy.wait_recv()

    load_d.wait()
    rates = dec_ref[...]
    tmp[...] = jnp.zeros_like(tmp)
    for k in range(CD // NG):
        tmp[NG * k : NG * (k + 1), 0:MODES] = rates
    rmc = jnp.transpose(tmp[...])[:MODES]
    for k in range(3):
        rates3[:, MODES * k : MODES * (k + 1)] = rates
    span = 2 * BL
    ahead = iota((MODES, span), 1).astype(F32)
    behind = span - ahead
    for g in range(NG):
        column = jnp.broadcast_to(rmc[:, g : g + 1], (MODES, span))
        pw[MODES * g : MODES * (g + 1), :] = jnp.exp(-(column * ahead))
        pt[MODES * g : MODES * (g + 1), :] = jnp.exp(-(column * behind))

    wide = jnp.broadcast_to(pt[:, 0:1], (NG * MODES, 2 * CD))
    half_decay = jnp.exp(-(float(TOK // 2) * rmc))
    blocks = TOK // 2 // span

    def summary(ref, powers, order):
        hi, lo = split(powers[...])
        total = None
        for b in order:
            both = jnp.concatenate(
                [ref[b * span : (b + 1) * span, :], ref[TOK // 2 + b * span : TOK // 2 + (b + 1) * span, :]],
                axis=1,
            )
            part = nn(hi, both) + nn(lo, both)
            total = part if total is None else part + wide * total
        return extract(total[:, :CD]), extract(total[:, CD:])

    load_y.wait()
    first, second = summary(y, pw, range(blocks - 1, -1, -1))
    s1[0] = first + half_decay * second
    load_x.wait()
    load_r.wait()
    load_k.wait()
    first, second = summary(x, pt, range(blocks))
    t1[0] = second + half_decay * first

    def regroup(src, dst, step):
        for r in range(0, BL, step):
            for g, piece in enumerate(exchange([src[b * BL + r : b * BL + r + step, :] for b in range(NB)])):
                dst[g, r : r + step, :] = piece

    regroup(y, yn, 32)
    regroup(x, xn, 32)

    pl.semaphore_wait(barrier, len(everyone))
    c_s1 = send(s1, quad_peers, 0)
    c_t1 = send(t1, quad_peers, 4)

    row_c, lane_c = iota((BL, BL), 0), iota((BL, BL), 1)
    flip = jnp.where(lane_c + row_c == BL - 1, 1.0, 0.0).astype(BF16)
    for g in range(NG):
        gs = slice(MODES * g, MODES * (g + 1))
        ph, pl_ = split(pw[gs, :BL])
        th, tl = split(pt[gs, BL:])
        yq, xq = yn[g], xn[g]
        part = nn(jnp.concatenate([ph, pl_], axis=0), yq)
        zs[gs, :] = part[:MODES] + part[MODES:]
        part = nn(jnp.concatenate([flip, th, tl], axis=0), xq)
        tb[gs, :] = part[BL : BL + MODES] + part[BL + MODES :]
        gram = nt(part[:BL].astype(BF16), yq)
        gram = pltpu.roll(gram, 1, 1, stride=1, stride_axis=0)
        lags[g : g + 1, :] = jnp.sum(jnp.where(lane_c <= row_c, gram, 0.0), axis=0, keepdims=True)

    block_of = iota((NG * MODES, CD), 1) % NB
    run = zs[...]
    decay = jnp.broadcast_to(pw[:, BL : BL + 1], (NG * MODES, CD))
    for k in (1, 2, 4, 8):
        run = run + jnp.where(block_of + k < NB, decay * pltpu.roll(run, CD - k, 1), 0.0)
        decay = decay * decay
    run = jnp.where(block_of + 1 < NB, pltpu.roll(run, CD - 1, 1), 0.0)
    after[...] = run
    h = jnp.zeros((MODES, CD), F32)
    for g in range(NG):
        gs = slice(MODES * g, MODES * (g + 1))
        terms = pw[gs, :BL] * lags[g : g + 1, :] + tb[gs, :] * after[gs, :]
        column = jnp.sum(terms, axis=1, keepdims=True)
        h = h + jnp.where(iota((MODES, CD), 1) == g, column, 0.0)
    skip_sum = jnp.zeros((BL, CD), F32)
    for b in range(NB):
        rows = slice(b * BL, (b + 1) * BL)
        skip_sum = skip_sum + x[rows, :].astype(F32) * y[rows, :].astype(F32)
    skip_sum = jnp.sum(skip_sum, axis=0, keepdims=True)
    gz[0] = pack(h) + jnp.where(iota((8, CD), 0) == 2, skip_sum, 0.0)
    c_gz = send(gz, z_peers, 8)

    dev = jnp.exp(-(float(TOK) * rmc))
    quad = jnp.exp(-(float(TOK * NQ) * rmc))
    slab = jnp.exp(-(float(TOK * NQ * NZ) * rmc))
    load_s1 = lambda i: s1[lax.rem(i - q + NQ, NQ)]
    arrive(c_s1)
    s2[0] = suffix(load_s1, NQ, dev)
    c_s2 = send(s2, z_peers, 16)
    arrive(c_t1)
    p1, tq = pairs(load_s1, lambda i: t1[lax.rem(i - q + NQ, NQ)], NQ, dev)
    t2[0, 0:16] = tq
    t2[0, 16:24] = pack(p1)
    c_t2 = send(t2, z_peers, 24)

    twice = 2.0 * rates
    series = twice * (1.0 - twice / 2 * (1.0 - twice / 3 * (1.0 - twice / 4 * (
        1.0 - twice / 5 * (1.0 - twice / 6 * (1.0 - twice / 7 * (1.0 - twice / 8)))))))
    norm = jnp.sqrt(jnp.where(twice < 0.25, series, 1.0 - jnp.exp(-twice)))
    coef = res_ref[...] * norm
    for k in range(CD // NG):
        tmp[NG * k : NG * (k + 1), 0:MODES] = coef
    cmc_ref[...] = jnp.transpose(tmp[...])[:MODES]

    third = iota((BL, 3 * MODES), 1) // MODES
    left = (BL - iota((BL, 3 * MODES), 0)).astype(F32)

    def local_one(g):
        gs = slice(MODES * g, MODES * (g + 1))
        yq = yn[g]
        column = jnp.broadcast_to(cmc_ref[:, g : g + 1], (MODES, CD))
        taps = jnp.sum(column * pw[gs, :BL], axis=0, keepdims=True)
        toep = pltpu.roll(jnp.broadcast_to(taps, (BL, BL)), 0, 1, stride=1, stride_axis=0)
        th, tl = split(jnp.where(lane_c >= row_c, toep, 0.0))
        ah, al = split(column * after[gs, :])
        reach = jnp.exp(-(left * rates3[g : g + 1, :]))
        rh = reach.astype(BF16).astype(F32)
        reach = jnp.where(third == 1, reach - rh, rh).astype(BF16)
        on[g] = nn(
            jnp.concatenate([th, tl], axis=1), jnp.concatenate([yq, yq], axis=0)
        ) + nn(reach, jnp.concatenate([ah, ah, al], axis=0))

    for g in range(NG):
        local_one(g)

    skip_row = skip_ref[...].reshape(1, CD)
    for r in range(0, BL, 16):
        for b, piece in enumerate(exchange([on[g, r : r + 16, :] for g in range(NG)])):
            rows = slice(b * BL + r, b * BL + r + 16)
            loc[rows, :] = piece + skip_row * y[rows, :].astype(F32)

    def add_up(buf, count):
        total = buf[0]
        for k in range(1, count):
            total = total + buf[k]
        return total

    own_row = iota((8, CD), 0) == 2
    arrive(c_gz)
    gy[0] = add_up(gz, NZ)
    c_gy = send(gy, y_peers + o_peers, 32)

    hl = TOK // 2
    column = jnp.concatenate(
        [jnp.broadcast_to(rmc[:, g : g + 1], (MODES, CD)) for g in range(NG)], axis=0
    )
    rowr = jnp.transpose(column)[0:1]
    for b in range(hl // BL):
        rows = slice(b * BL, (b + 1) * BL)
        away = (hl - b * BL - iota((BL, NG * MODES), 0)).astype(F32)
        qh[rows, :], ql[rows, :] = split(jnp.exp(-(away * rowr)))

    arrive(c_s2)
    load_s2 = lambda i: s2[lax.rem(i - z + NZ, NZ)]
    s3[0] = suffix(load_s2, NZ, quad)
    c_s3 = send(s3, y_peers, 40)
    arrive(c_t2)
    p2, ty = pairs(load_s2, lambda i: t2[lax.rem(i - z + NZ, NZ), 0:16], NZ, quad)
    g2 = pack(p2)
    for k in range(NZ):
        g2 = g2 + t2[k, 16:24]
    m3[0, 0:16] = s3[0]
    m3[0, 16:32] = ty
    m3[0, 32:40] = g2
    c_m3 = send(m3, y_peers + o_peers, 44)

    arrive(c_gy)
    both_halves = add_up(gy, 2 * NY)
    own_half = gy[0] + gy[1] + gy[2] + gy[3]
    gq[0] = jnp.where(own_row, own_half, both_halves)
    c_gq = send(gq, quad_peers, 52)

    arrive(c_s3)
    one = jnp.ones((MODES, CD), F32)
    zero = jnp.zeros((MODES, CD), F32)
    inc_y, w = zero, one
    for k in range(1, NY):
        inc_y = inc_y + jnp.where(yy + k < NY, w, zero) * s3[k]
        w = w * slab
    inc_z, w = zero, one
    for k in range(1, NZ):
        inc_z = inc_z + jnp.where(z + k < NZ, w, zero) * s2[k]
        w = w * quad
    inc_q, w = zero, one
    for k in range(1, NQ):
        inc_q = inc_q + jnp.where(q + k < NQ, w, zero) * s1[k]
        w = w * dev
    to_slab = jnp.exp(-(((NZ - 1 - z) * (TOK * NQ)).astype(F32) * rmc))
    to_quad = jnp.exp(-(((NQ - 1 - q) * TOK).astype(F32) * rmc))
    inc = inc_q + to_quad * (inc_z + to_slab * inc_y)

    late = cmc_ref[...] * inc
    early = late * half_decay
    group_of = iota((MODES, CD), 1) % NG

    def spread(v):
        return jnp.concatenate([jnp.where(group_of == g, v, 0.0) for g in range(NG)], axis=0)

    def both(v, u):
        return jnp.concatenate([spread(v), spread(u)], axis=1).astype(BF16)

    eh = early.astype(BF16).astype(F32)
    lh = late.astype(BF16).astype(F32)
    a_hi = both(eh, lh)
    a_lo = both(early - eh, late - lh)
    arrived = jnp.concatenate([a_hi, a_lo, a_hi], axis=0)
    step = 2 * BL
    for r in range(0, hl, step):
        rows, rows2 = slice(r, r + step), slice(hl + r, hl + r + step)
        hi, lo = qh[rows, :], ql[rows, :]
        add = nn(jnp.concatenate([hi, hi, lo], axis=1), arrived)
        outb[rows, :] = (loc[rows, :] + add[:, :CD]).astype(BF16)
        outb[rows2, :] = (loc[rows2, :] + add[:, CD:]).astype(BF16)

    arrive(c_gq)
    base = add_up(gq, NQ)
    total_len = TOK * NQ * NZ * NY
    sg_ref[...] = (base[2:3] * (1.0 / math.sqrt(total_len))).reshape(CD)
    arrive(c_m3)

    def load_y3(lo, base):
        return lambda i: m3[base + lax.rem(i - yy + NY, NY), lo : lo + 16]

    p3, _ = pairs(load_y3(0, 0), load_y3(16, 0), NY, slab)
    p4, _ = pairs(load_y3(0, NY), load_y3(16, NY), NY, slab)
    for k in range(2 * NY):
        base = base + m3[k, 32:40]
    grads = fold(unpack(base) + p3 + p4)
    tmp[...] = jnp.zeros_like(tmp)
    tmp[0:MODES, :] = grads
    turned = jnp.transpose(tmp[...])[0:NG, 0:MODES]
    rg_ref[...] = turned * norm * (1.0 / math.sqrt(GROUP * total_len))

    for copy in sent:
        copy.wait_send()


def deliver(a, b, c, to_a, to_b, to_c, sems):
    copies = [
        pltpu.make_async_copy(src, dst, sems.at[i])
        for i, (src, dst) in enumerate(((a, to_a), (b, to_b), (c, to_c)))
    ]
    for copy in copies:
        copy.start()
    for copy in copies:
        copy.wait()


def shards(inputs, cotangent, residues, decay_rates, skip_weight):
    vmem = pl.BlockSpec(memory_space=pltpu.VMEM)
    hbm = pl.BlockSpec(memory_space=pltpu.HBM)
    near = pl.pallas_call(
        kernel,
        out_shape=(
            pltpu.VMEM((TOK, CD), BF16),
            pltpu.VMEM((NG, MODES), F32),
            pltpu.VMEM((CD,), F32),
        ),
        in_specs=[hbm] * 5,
        out_specs=(vmem, vmem, vmem),
        scratch_shapes=[
            pltpu.VMEM((TOK, CD), BF16),
            pltpu.VMEM((TOK, CD), BF16),
            pltpu.VMEM((NG, MODES), F32),
            pltpu.VMEM((NG, MODES), F32),
            pltpu.VMEM((CD,), F32),
            pltpu.VMEM((NG, BL, CD), BF16),
            pltpu.VMEM((NG, BL, CD), BF16),
            pltpu.VMEM((CD, CD), F32),
            pltpu.VMEM((MODES, CD), F32),
            pltpu.VMEM((NG, 3 * MODES), F32),
            pltpu.VMEM((NG * MODES, 2 * BL), F32),
            pltpu.VMEM((NG * MODES, 2 * BL), F32),
            pltpu.VMEM((NG * MODES, CD), F32),
            pltpu.VMEM((NG * MODES, CD), F32),
            pltpu.VMEM((NG, BL), F32),
            pltpu.VMEM((NG * MODES, CD), F32),
            pltpu.VMEM((NG, BL, CD), F32),
            pltpu.VMEM((TOK, CD), F32),
            pltpu.VMEM((TOK // 2, NG * MODES), BF16),
            pltpu.VMEM((TOK // 2, NG * MODES), BF16),
            pltpu.VMEM((NQ, MODES, CD), F32),
            pltpu.VMEM((NQ, MODES, CD), F32),
            pltpu.VMEM((NZ, MODES, CD), F32),
            pltpu.VMEM((NZ, 24, CD), F32),
            pltpu.VMEM((NY, MODES, CD), F32),
            pltpu.VMEM((2 * NY, 40, CD), F32),
            pltpu.VMEM((NZ, 8, CD), F32),
            pltpu.VMEM((2 * NY, 8, CD), F32),
            pltpu.VMEM((NQ, 8, CD), F32),
            pltpu.SemaphoreType.DMA((5,)),
            pltpu.SemaphoreType.DMA((56,)),
            pltpu.SemaphoreType.DMA((56,)),
        ],
        compiler_params=pltpu.CompilerParams(
            collective_id=0, has_side_effects=True, vmem_limit_bytes=32 << 20
        ),
    )(*[pltpu.with_memory_space_constraint(v, pltpu.HBM) for v in (inputs, cotangent, residues, decay_rates, skip_weight)])
    return pl.pallas_call(
        deliver,
        out_shape=(
            jax.ShapeDtypeStruct((TOK, CD), BF16),
            jax.ShapeDtypeStruct((NG, MODES), F32),
            jax.ShapeDtypeStruct((CD,), F32),
        ),
        in_specs=[vmem, vmem, vmem],
        out_specs=(hbm, hbm, hbm),
        scratch_shapes=[pltpu.SemaphoreType.DMA((3,))],
    )(*[pltpu.with_memory_space_constraint(v, pltpu.VMEM) for v in near])


def solution(mesh):
    placed = (P("seq", "chan"), P("seq", "chan"), P(), P(), P("chan"))
    return jax.shard_map(
        shards,
        mesh=mesh,
        in_specs=placed,
        out_specs=(P("seq", "chan"), P(), P("chan")),
        check_vma=False,
    )
```

```python
import math

import jax
import jax.numpy as jnp
from jax import lax
from jax.experimental import pallas as pl
from jax.experimental.pallas import tpu as pltpu
from jax.sharding import PartitionSpec as P

MESH = pl.DeviceIdType.MESH
F32 = jnp.float32
BF16 = jnp.bfloat16
NG = 16
MODES = 16
GROUP = 16
TOK = 2048
CD = 128
BL = 128
NB = TOK // BL
NQ, NZ, NY = 4, 8, 4


def split(v):
    hi = v.astype(BF16)
    return hi, (v - hi.astype(F32)).astype(BF16)


def nn(a, b):
    return lax.dot_general(a, b, (((1,), (0,)), ((), ())), preferred_element_type=F32)


def nt(a, b):
    return lax.dot_general(a, b, (((1,), (1,)), ((), ())), preferred_element_type=F32)


def iota(shape, dim):
    return lax.broadcasted_iota(jnp.int32, shape, dim)


def fold(h):
    h = h + pltpu.roll(h, 64, 1)
    h = h + pltpu.roll(h, 32, 1)
    return h + pltpu.roll(h, 16, 1)


def pack(h):
    h = fold(h)
    keep = iota((8, CD), 1) // 16 == iota((8, CD), 0)
    first = jnp.sum(jnp.where(keep, h[:8], 0.0), axis=0, keepdims=True)
    second = jnp.sum(jnp.where(keep, h[8:], 0.0), axis=0, keepdims=True)
    row = iota((8, CD), 0)
    return jnp.where(row == 0, first, jnp.where(row == 1, second, 0.0))


def unpack(tile):
    keep = iota((8, CD), 1) // 16 == iota((8, CD), 0)
    return jnp.concatenate(
        [jnp.where(keep, tile[0:1], 0.0), jnp.where(keep, tile[1:2], 0.0)], axis=0
    )


def gather_sum(parts):
    bit_of = iota(parts[0].shape, 1)
    for k in (8, 4, 2, 1):
        keep = (bit_of & k) == 0
        parts = [
            jnp.where(keep, low + pltpu.roll(low, CD - k, 1), high + pltpu.roll(high, k, 1))
            for low, high in zip(parts[:k], parts[k:])
        ]
    return parts[0]


def suffix(load_s, count, w):
    acc = load_s(count - 1)
    for i in range(count - 2, -1, -1):
        acc = load_s(i) + w * acc
    return acc


def pairs(load_s, load_t, count, w):
    acc = load_t(0)
    total = None
    for i in range(1, count):
        term = acc * load_s(i)
        total = term if total is None else total + term
        acc = load_t(i) + w * acc
    return total, acc


def exchange(blocks):
    bit_of = iota(blocks[0].shape, 1)
    for k in (1, 2, 4, 8):
        keep = (bit_of & k) == 0
        for i in range(NG):
            if not i & k:
                low, high = blocks[i], blocks[i | k]
                blocks[i] = jnp.where(keep, low, pltpu.roll(high, k, 1))
                blocks[i | k] = jnp.where(keep, pltpu.roll(low, CD - k, 1), high)
    return blocks


def kernel(
    x_hbm, y_hbm, res_hbm, dec_hbm, skip_hbm,
    outb, rg_ref, sg_ref,
    x, y, res_ref, dec_ref, skip_ref, xn, yn, tmp, cmc_ref, rates3, pw, pt, ws, wt, zs, tb, lags, after, on, xr, loc, qh, ql,
    m1, m2, m3, gz, gq,
    load_sem, send_sem, recv_sem,
):
    me = lax.axis_index("seq")
    half = lax.axis_index("chan")
    q = lax.rem(me, NQ)
    z = lax.rem(me // NQ, NZ)
    yy = me // (NQ * NZ)

    def at(y_i, z_i, q_i, h_i):
        return {"seq": (y_i * NZ + z_i) * NQ + q_i, "chan": h_i}

    quad_peers = [(k, at(yy, z, lax.rem(q + NQ - k, NQ), half)) for k in (2, 3, 1)]
    z_peers = [(k, at(yy, lax.rem(z + NZ - k, NZ), q, half)) for k in (4, 3, 5, 2, 6, 1, 7)]
    y_peers = [(k, at(lax.rem(yy + NY - k, NY), z, q, half)) for k in (2, 1, 3)]
    o_peers = [(NY + k, at(lax.rem(yy + NY - k, NY), z, q, 1 - half)) for k in (2, 1, 3, 0)]

    load_y = pltpu.make_async_copy(y_hbm, y, load_sem.at[0])
    load_x = pltpu.make_async_copy(x_hbm, x, load_sem.at[1])
    load_r = pltpu.make_async_copy(res_hbm, res_ref, load_sem.at[2])
    load_d = pltpu.make_async_copy(dec_hbm, dec_ref, load_sem.at[3])
    load_k = pltpu.make_async_copy(skip_hbm, skip_ref, load_sem.at[4])
    barrier = pltpu.get_barrier_semaphore()
    everyone = z_peers + o_peers + y_peers + quad_peers
    for _, peer in everyone:
        pl.semaphore_signal(barrier, inc=1, device_id=peer, device_id_type=MESH)
    load_d.start()
    load_y.start()
    load_x.start()
    load_r.start()
    load_k.start()

    sent = []

    def send(buf, peers, sem):
        for slot, peer in peers:
            pltpu.make_async_remote_copy(
                src_ref=buf.at[0],
                dst_ref=buf.at[slot],
                send_sem=send_sem.at[sem],
                recv_sem=recv_sem.at[sem],
                device_id=peer,
                device_id_type=MESH,
            ).start()
        slots = [slot for slot, _ in peers]
        area = buf.at[min(slots) : max(slots) + 1]
        sent.append(pltpu.make_async_copy(area, area, send_sem.at[sem]))
        return pltpu.make_async_copy(area, area, recv_sem.at[sem])

    def arrive(copies):
        copies.wait()

    load_d.wait()
    rates = dec_ref[...]
    tmp[...] = jnp.zeros_like(tmp)
    for k in range(CD // NG):
        tmp[NG * k : NG * (k + 1), 0:MODES] = rates
    rmc = jnp.transpose(tmp[...])[:MODES]
    for k in range(3):
        rates3[:, MODES * k : MODES * (k + 1)] = rates
    span = 2 * BL
    ahead = iota((MODES, span), 1).astype(F32)
    behind = span - ahead
    in_block = (BL * (iota((MODES, CD), 1) % NB)).astype(F32)
    out_block = float(BL * (NB - 1)) - in_block
    for g in range(NG):
        column = jnp.broadcast_to(rmc[:, g : g + 1], (MODES, span))
        pw[MODES * g : MODES * (g + 1), :] = jnp.exp(-(column * ahead))
        pt[MODES * g : MODES * (g + 1), :] = jnp.exp(-(column * behind))
        ws[MODES * g : MODES * (g + 1), :] = jnp.exp(-(column[:, :CD] * in_block))
        wt[MODES * g : MODES * (g + 1), :] = jnp.exp(-(column[:, :CD] * out_block))

    def regroup(src, dst, step):
        for r in range(0, BL, step):
            for g, piece in enumerate(exchange([src[b * BL + r : b * BL + r + step, :] for b in range(NB)])):
                dst[g, r : r + step, :] = piece

    row_c, lane_c = iota((BL, BL), 0), iota((BL, BL), 1)
    flip = jnp.where(lane_c + row_c == BL - 1, 1.0, 0.0).astype(BF16)
    half_decay = jnp.exp(-(float(TOK // 2) * rmc))
    load_y.wait()
    regroup(y, yn, 32)
    parts = []
    for g in range(NG):
        gs = slice(MODES * g, MODES * (g + 1))
        hi, lo = split(pw[gs, :BL])
        part = nn(jnp.concatenate([hi, lo], axis=0), yn[g])
        part = part[:MODES] + part[MODES:]
        zs[gs, :] = part
        parts.append(part * ws[gs, :])
    m1[0, 0:16] = gather_sum(parts)
    load_x.wait()
    load_r.wait()
    load_k.wait()
    regroup(x, xn, 32)
    parts = []
    for g in range(NG):
        gs = slice(MODES * g, MODES * (g + 1))
        hi, lo = split(pt[gs, BL:])
        part = nn(jnp.concatenate([flip, hi, lo], axis=0), xn[g])
        xr[g] = part[:BL].astype(BF16)
        part = part[BL : BL + MODES] + part[BL + MODES :]
        tb[gs, :] = part
        parts.append(part * wt[gs, :])
    m1[0, 16:32] = gather_sum(parts)

    pl.semaphore_wait(barrier, len(everyone))
    c_m1 = send(m1, quad_peers, 0)

    for g in range(NG):
        gram = nt(xr[g], yn[g])
        gram = pltpu.roll(gram, 1, 1, stride=1, stride_axis=0)
        lags[g : g + 1, :] = jnp.sum(jnp.where(lane_c <= row_c, gram, 0.0), axis=0, keepdims=True)

    block_of = iota((NG * MODES, CD), 1) % NB
    run = zs[...]
    decay = jnp.broadcast_to(pw[:, BL : BL + 1], (NG * MODES, CD))
    for k in (1, 2, 4, 8):
        run = run + jnp.where(block_of + k < NB, decay * pltpu.roll(run, CD - k, 1), 0.0)
        decay = decay * decay
    run = jnp.where(block_of + 1 < NB, pltpu.roll(run, CD - 1, 1), 0.0)
    after[...] = run
    h = jnp.zeros((MODES, CD), F32)
    for g in range(NG):
        gs = slice(MODES * g, MODES * (g + 1))
        terms = pw[gs, :BL] * lags[g : g + 1, :] + tb[gs, :] * after[gs, :]
        column = jnp.sum(terms, axis=1, keepdims=True)
        h = h + jnp.where(iota((MODES, CD), 1) == g, column, 0.0)
    skip_sum = jnp.zeros((BL, CD), F32)
    for b in range(NB):
        rows = slice(b * BL, (b + 1) * BL)
        skip_sum = skip_sum + x[rows, :].astype(F32) * y[rows, :].astype(F32)
    skip_sum = jnp.sum(skip_sum, axis=0, keepdims=True)
    gz[0] = pack(h) + jnp.where(iota((8, CD), 0) == 2, skip_sum, 0.0)
    c_gz = send(gz, z_peers, 1)

    dev = jnp.exp(-(float(TOK) * rmc))
    quad = jnp.exp(-(float(TOK * NQ) * rmc))
    slab = jnp.exp(-(float(TOK * NQ * NZ) * rmc))
    arrive(c_m1)
    load1 = lambda lo: lambda i: m1[lax.rem(i - q + NQ, NQ), lo : lo + 16]
    m2[0, 0:16] = suffix(load1(0), NQ, dev)
    p1, tq = pairs(load1(0), load1(16), NQ, dev)
    m2[0, 16:32] = tq
    m2[0, 32:40] = pack(p1)
    c_m2 = send(m2, z_peers, 2)

    twice = 2.0 * rates
    series = twice * (1.0 - twice / 2 * (1.0 - twice / 3 * (1.0 - twice / 4 * (
        1.0 - twice / 5 * (1.0 - twice / 6 * (1.0 - twice / 7 * (1.0 - twice / 8)))))))
    norm = jnp.sqrt(jnp.where(twice < 0.25, series, 1.0 - jnp.exp(-twice)))
    coef = res_ref[...] * norm
    for k in range(CD // NG):
        tmp[NG * k : NG * (k + 1), 0:MODES] = coef
    cmc_ref[...] = jnp.transpose(tmp[...])[:MODES]

    third = iota((BL, 3 * MODES), 1) // MODES
    left = (BL - iota((BL, 3 * MODES), 0)).astype(F32)

    def local_one(g):
        gs = slice(MODES * g, MODES * (g + 1))
        yq = yn[g]
        column = jnp.broadcast_to(cmc_ref[:, g : g + 1], (MODES, CD))
        taps = jnp.sum(column * pw[gs, :BL], axis=0, keepdims=True)
        toep = pltpu.roll(jnp.broadcast_to(taps, (BL, BL)), 0, 1, stride=1, stride_axis=0)
        th, tl = split(jnp.where(lane_c >= row_c, toep, 0.0))
        ah, al = split(column * after[gs, :])
        reach = jnp.exp(-(left * rates3[g : g + 1, :]))
        rh = reach.astype(BF16).astype(F32)
        reach = jnp.where(third == 1, reach - rh, rh).astype(BF16)
        on[g] = nn(
            jnp.concatenate([th, tl], axis=1), jnp.concatenate([yq, yq], axis=0)
        ) + nn(reach, jnp.concatenate([ah, ah, al], axis=0))

    for g in range(NG):
        local_one(g)

    skip_row = skip_ref[...].reshape(1, CD)
    for r in range(0, BL, 16):
        for b, piece in enumerate(exchange([on[g, r : r + 16, :] for g in range(NG)])):
            rows = slice(b * BL + r, b * BL + r + 16)
            loc[rows, :] = piece + skip_row * y[rows, :].astype(F32)

    def add_up(buf, count):
        total = buf[0]
        for k in range(1, count):
            total = total + buf[k]
        return total

    arrive(c_gz)
    gq[0] = add_up(gz, NZ)
    c_gq = send(gq, quad_peers, 3)

    hl = TOK // 2
    column = jnp.concatenate(
        [jnp.broadcast_to(rmc[:, g : g + 1], (MODES, CD)) for g in range(NG)], axis=0
    )
    rowr = jnp.transpose(column)[0:1]
    for b in range(hl // BL):
        rows = slice(b * BL, (b + 1) * BL)
        away = (hl - b * BL - iota((BL, NG * MODES), 0)).astype(F32)
        qh[rows, :], ql[rows, :] = split(jnp.exp(-(away * rowr)))

    arrive(c_gq)
    lag_part = add_up(gq, NQ)
    arrive(c_m2)
    load2 = lambda lo: lambda i: m2[lax.rem(i - z + NZ, NZ), lo : lo + 16]
    m3[0, 0:16] = suffix(load2(0), NZ, quad)
    p2, ty = pairs(load2(0), load2(16), NZ, quad)
    m3[0, 16:32] = ty
    lag_part = lag_part + pack(p2)
    for k in range(NZ):
        lag_part = lag_part + m2[k, 32:40]
    m3[0, 32:40] = lag_part
    c_o3 = send(m3, o_peers, 4)
    c_m3 = send(m3, y_peers, 5)

    arrive(c_m3)
    one = jnp.ones((MODES, CD), F32)
    zero = jnp.zeros((MODES, CD), F32)
    inc_y, w = zero, one
    for k in range(1, NY):
        inc_y = inc_y + jnp.where(yy + k < NY, w, zero) * m3[k, 0:16]
        w = w * slab
    inc_z, w = zero, one
    for k in range(1, NZ):
        inc_z = inc_z + jnp.where(z + k < NZ, w, zero) * m2[k, 0:16]
        w = w * quad
    inc_q, w = zero, one
    for k in range(1, NQ):
        inc_q = inc_q + jnp.where(q + k < NQ, w, zero) * m1[k, 0:16]
        w = w * dev
    to_slab = jnp.exp(-(((NZ - 1 - z) * (TOK * NQ)).astype(F32) * rmc))
    to_quad = jnp.exp(-(((NQ - 1 - q) * TOK).astype(F32) * rmc))
    inc = inc_q + to_quad * (inc_z + to_slab * inc_y)

    late = cmc_ref[...] * inc
    early = late * half_decay
    group_of = iota((MODES, CD), 1) % NG

    def spread(v):
        return jnp.concatenate([jnp.where(group_of == g, v, 0.0) for g in range(NG)], axis=0)

    def both(v, u):
        return jnp.concatenate([spread(v), spread(u)], axis=1).astype(BF16)

    eh = early.astype(BF16).astype(F32)
    lh = late.astype(BF16).astype(F32)
    a_hi = both(eh, lh)
    a_lo = both(early - eh, late - lh)
    arrived = jnp.concatenate([a_hi, a_lo, a_hi], axis=0)
    step = 2 * BL
    for r in range(0, hl, step):
        rows, rows2 = slice(r, r + step), slice(hl + r, hl + r + step)
        hi, lo = qh[rows, :], ql[rows, :]
        add = nn(jnp.concatenate([hi, hi, lo], axis=1), arrived)
        outb[rows, :] = (loc[rows, :] + add[:, :CD]).astype(BF16)
        outb[rows2, :] = (loc[rows2, :] + add[:, CD:]).astype(BF16)

    for copy in sent[:-2]:
        copy.wait()
    total_len = TOK * NQ * NZ * NY
    load3 = lambda lo, base: lambda i: m3[base + lax.rem(i - yy + NY, NY), lo : lo + 16]
    p3, _ = pairs(load3(0, 0), load3(16, 0), NY, slab)
    base = m3[0, 32:40] + m3[1, 32:40] + m3[2, 32:40] + m3[3, 32:40]
    sg_ref[...] = (base[2:3] * (1.0 / math.sqrt(total_len))).reshape(CD)
    arrive(c_o3)
    p4, _ = pairs(load3(0, NY), load3(16, NY), NY, slab)
    base = base + m3[4, 32:40] + m3[5, 32:40] + m3[6, 32:40] + m3[7, 32:40]
    grads = fold(unpack(base) + p3 + p4)
    tmp[...] = jnp.zeros_like(tmp)
    tmp[0:MODES, :] = grads
    turned = jnp.transpose(tmp[...])[0:NG, 0:MODES]
    rg_ref[...] = turned * norm * (1.0 / math.sqrt(GROUP * total_len))

    for copy in sent[-2:]:
        copy.wait()


def deliver(a, b, c, to_a, to_b, to_c, sems):
    copies = [
        pltpu.make_async_copy(src, dst, sems.at[i])
        for i, (src, dst) in enumerate(((a, to_a), (b, to_b), (c, to_c)))
    ]
    for copy in copies:
        copy.start()
    for copy in copies:
        copy.wait()


def shards(inputs, cotangent, residues, decay_rates, skip_weight):
    vmem = pl.BlockSpec(memory_space=pltpu.VMEM)
    hbm = pl.BlockSpec(memory_space=pltpu.HBM)
    near = pl.pallas_call(
        kernel,
        out_shape=(
            pltpu.VMEM((TOK, CD), BF16),
            pltpu.VMEM((NG, MODES), F32),
            pltpu.VMEM((CD,), F32),
        ),
        in_specs=[hbm] * 5,
        out_specs=(vmem, vmem, vmem),
        scratch_shapes=[
            pltpu.VMEM((TOK, CD), BF16),
            pltpu.VMEM((TOK, CD), BF16),
            pltpu.VMEM((NG, MODES), F32),
            pltpu.VMEM((NG, MODES), F32),
            pltpu.VMEM((CD,), F32),
            pltpu.VMEM((NG, BL, CD), BF16),
            pltpu.VMEM((NG, BL, CD), BF16),
            pltpu.VMEM((CD, CD), F32),
            pltpu.VMEM((MODES, CD), F32),
            pltpu.VMEM((NG, 3 * MODES), F32),
            pltpu.VMEM((NG * MODES, 2 * BL), F32),
            pltpu.VMEM((NG * MODES, 2 * BL), F32),
            pltpu.VMEM((NG * MODES, CD), F32),
            pltpu.VMEM((NG * MODES, CD), F32),
            pltpu.VMEM((NG * MODES, CD), F32),
            pltpu.VMEM((NG * MODES, CD), F32),
            pltpu.VMEM((NG, BL), F32),
            pltpu.VMEM((NG * MODES, CD), F32),
            pltpu.VMEM((NG, BL, CD), F32),
            pltpu.VMEM((NG, BL, CD), BF16),
            pltpu.VMEM((TOK, CD), F32),
            pltpu.VMEM((TOK // 2, NG * MODES), BF16),
            pltpu.VMEM((TOK // 2, NG * MODES), BF16),
            pltpu.VMEM((NQ, 32, CD), F32),
            pltpu.VMEM((NZ, 40, CD), F32),
            pltpu.VMEM((2 * NY, 40, CD), F32),
            pltpu.VMEM((NZ, 8, CD), F32),
            pltpu.VMEM((NQ, 8, CD), F32),
            pltpu.SemaphoreType.DMA((5,)),
            pltpu.SemaphoreType.DMA((6,)),
            pltpu.SemaphoreType.DMA((6,)),
        ],
        compiler_params=pltpu.CompilerParams(
            collective_id=0, has_side_effects=True, vmem_limit_bytes=32 << 20
        ),
    )(*[pltpu.with_memory_space_constraint(v, pltpu.HBM) for v in (inputs, cotangent, residues, decay_rates, skip_weight)])
    return pl.pallas_call(
        deliver,
        out_shape=(
            jax.ShapeDtypeStruct((TOK, CD), BF16),
            jax.ShapeDtypeStruct((NG, MODES), F32),
            jax.ShapeDtypeStruct((CD,), F32),
        ),
        in_specs=[vmem, vmem, vmem],
        out_specs=(hbm, hbm, hbm),
        scratch_shapes=[pltpu.SemaphoreType.DMA((3,))],
    )(*[pltpu.with_memory_space_constraint(v, pltpu.VMEM) for v in near])


def solution(mesh):
    placed = (P("seq", "chan"), P("seq", "chan"), P(), P(), P("chan"))
    return jax.shard_map(
        shards,
        mesh=mesh,
        in_specs=placed,
        out_specs=(P("seq", "chan"), P(), P("chan")),
        check_vma=False,
    )
```

```python
import math

import jax
import jax.numpy as jnp
from jax import lax
from jax.experimental import pallas as pl
from jax.experimental.pallas import tpu as pltpu
from jax.sharding import PartitionSpec as P

MESH = pl.DeviceIdType.MESH
F32 = jnp.float32
BF16 = jnp.bfloat16
NG = 16
MODES = 16
GROUP = 16
TOK = 2048
CD = 128
BL = 128
NB = TOK // BL
NQ, NZ, NY = 4, 8, 4


def split(v):
    hi = v.astype(BF16)
    return hi, (v - hi.astype(F32)).astype(BF16)


def nn(a, b):
    return lax.dot_general(a, b, (((1,), (0,)), ((), ())), preferred_element_type=F32)


def nt(a, b):
    return lax.dot_general(a, b, (((1,), (1,)), ((), ())), preferred_element_type=F32)


def iota(shape, dim):
    return lax.broadcasted_iota(jnp.int32, shape, dim)


def fold(h):
    h = h + pltpu.roll(h, 64, 1)
    h = h + pltpu.roll(h, 32, 1)
    return h + pltpu.roll(h, 16, 1)


def pack(h):
    h = fold(h)
    keep = iota((8, CD), 1) // 16 == iota((8, CD), 0)
    first = jnp.sum(jnp.where(keep, h[:8], 0.0), axis=0, keepdims=True)
    second = jnp.sum(jnp.where(keep, h[8:], 0.0), axis=0, keepdims=True)
    row = iota((8, CD), 0)
    return jnp.where(row == 0, first, jnp.where(row == 1, second, 0.0))


def unpack(tile):
    keep = iota((8, CD), 1) // 16 == iota((8, CD), 0)
    return jnp.concatenate(
        [jnp.where(keep, tile[0:1], 0.0), jnp.where(keep, tile[1:2], 0.0)], axis=0
    )


def extract(full):
    group_of = iota((MODES, CD), 1) % NG
    out = jnp.zeros((MODES, CD), F32)
    for g in range(NG):
        out = jnp.where(group_of == g, full[MODES * g : MODES * (g + 1)], out)
    return out


def swap_dot(bits):
    row, lane = iota((CD, CD), 0), iota((CD, CD), 1)
    same = ((row ^ lane) & ~(3 << bits)) == 0
    row_bits, lane_bits = (row >> bits) & 3, (lane >> bits) & 3
    return jnp.concatenate(
        [
            jnp.concatenate(
                [
                    jnp.where(same & (lane_bits == i) & (row_bits == j), 1.0, 0.0).astype(BF16)
                    for j in range(4)
                ],
                axis=1,
            )
            for i in range(4)
        ],
        axis=0,
    )


def suffix(load_s, count, w):
    acc = load_s(count - 1)
    for i in range(count - 2, -1, -1):
        acc = load_s(i) + w * acc
    return acc


def pairs(load_s, load_t, count, w):
    acc = load_t(0)
    total = None
    for i in range(1, count):
        term = acc * load_s(i)
        total = term if total is None else total + term
        acc = load_t(i) + w * acc
    return total, acc


def exchange(blocks):
    bit_of = iota(blocks[0].shape, 1)
    for k in (1, 2, 4, 8):
        keep = (bit_of & k) == 0
        for i in range(NG):
            if not i & k:
                low, high = blocks[i], blocks[i | k]
                blocks[i] = jnp.where(keep, low, pltpu.roll(high, k, 1))
                blocks[i | k] = jnp.where(keep, pltpu.roll(low, CD - k, 1), high)
    return blocks


def kernel(
    x_hbm, y_hbm, res_hbm, dec_hbm, skip_hbm,
    outb, rg_ref, sg_ref,
    x, y, res_ref, dec_ref, skip_ref, xn, yn, tmp, cmc_ref, rates3, pw, pt, lags, ab, after, on, mid, swap, loc, qh, ql,
    m1, m2, m3, gz, gq,
    load_sem, send_sem, recv_sem,
):
    me = lax.axis_index("seq")
    half = lax.axis_index("chan")
    q = lax.rem(me, NQ)
    z = lax.rem(me // NQ, NZ)
    yy = me // (NQ * NZ)

    def at(y_i, z_i, q_i, h_i):
        return {"seq": (y_i * NZ + z_i) * NQ + q_i, "chan": h_i}

    quad_peers = [(k, at(yy, z, lax.rem(q + NQ - k, NQ), half)) for k in (2, 3, 1)]
    z_peers = [(k, at(yy, lax.rem(z + NZ - k, NZ), q, half)) for k in (4, 3, 5, 2, 6, 1, 7)]
    y_peers = [(k, at(lax.rem(yy + NY - k, NY), z, q, half)) for k in (2, 1, 3)]
    o_peers = [(NY + k, at(lax.rem(yy + NY - k, NY), z, q, 1 - half)) for k in (2, 1, 3, 0)]

    load_y = pltpu.make_async_copy(y_hbm, y, load_sem.at[0])
    load_x = pltpu.make_async_copy(x_hbm, x, load_sem.at[1])
    load_r = pltpu.make_async_copy(res_hbm, res_ref, load_sem.at[2])
    load_d = pltpu.make_async_copy(dec_hbm, dec_ref, load_sem.at[3])
    load_k = pltpu.make_async_copy(skip_hbm, skip_ref, load_sem.at[4])
    load_d.start()
    load_y.start()
    load_x.start()
    barrier = pltpu.get_barrier_semaphore()
    everyone = z_peers + o_peers + y_peers + quad_peers
    for _, peer in everyone:
        pl.semaphore_signal(barrier, inc=1, device_id=peer, device_id_type=MESH)

    load_r.start()
    load_k.start()
    sent = []

    def send(buf, peers, sem):
        for slot, peer in peers:
            pltpu.make_async_remote_copy(
                src_ref=buf.at[0],
                dst_ref=buf.at[slot],
                send_sem=send_sem.at[sem],
                recv_sem=recv_sem.at[sem],
                device_id=peer,
                device_id_type=MESH,
            ).start()
        slots = [slot for slot, _ in peers]
        area = buf.at[min(slots) : max(slots) + 1]
        sent.append(pltpu.make_async_copy(area, area, send_sem.at[sem]))
        return pltpu.make_async_copy(area, area, recv_sem.at[sem])

    def arrive(copies):
        copies.wait()

    swap[0] = swap_dot(0)
    swap[1] = swap_dot(2)
    load_d.wait()
    rates = dec_ref[...]
    tmp[...] = jnp.zeros_like(tmp)
    for k in range(CD // NG):
        tmp[NG * k : NG * (k + 1), 0:MODES] = rates
    rmc = jnp.transpose(tmp[...])[:MODES]
    for k in range(3):
        rates3[:, MODES * k : MODES * (k + 1)] = rates
    ahead = iota((MODES, BL), 1).astype(F32)
    behind = BL - ahead
    for g in range(NG):
        column = jnp.broadcast_to(rmc[:, g : g + 1], (MODES, BL))
        pw[MODES * g : MODES * (g + 1), :] = jnp.exp(-(column * ahead))
        pt[MODES * g : MODES * (g + 1), :] = jnp.exp(-(column * behind))

    def regroup(src, dst, step):
        for r in range(0, BL, step):
            for g, piece in enumerate(exchange([src[b * BL + r : b * BL + r + step, :] for b in range(NB)])):
                dst[g, r : r + step, :] = piece

    block_decay = jnp.exp(-(float(BL) * rmc))
    half_decay = jnp.exp(-(float(TOK // 2) * rmc))

    def block_states(ref, powers):
        hi, lo = split(powers[...])
        rates_side = jnp.concatenate([hi, lo], axis=1)
        states = []
        for b in range(0, NB, 2):
            two = jnp.concatenate(
                [ref[b * BL : (b + 1) * BL, :], ref[(b + 1) * BL : (b + 2) * BL, :]], axis=1
            )
            full = nn(rates_side, jnp.concatenate([two, two], axis=0))
            states += [extract(full[:, :CD]), extract(full[:, CD:])]
        return states

    load_y.wait()
    run = jnp.zeros((MODES, CD), F32)
    behind_block = [None] * NB
    states = block_states(y, pw)
    for b in range(NB - 1, -1, -1):
        behind_block[b] = run
        ab[b] = run
        run = states[b] + block_decay * run
    m1[0, 0:16] = run
    load_x.wait()
    states = block_states(x, pt)
    run = states[0]
    cross = run * behind_block[0]
    for b in range(1, NB):
        cross = cross + states[b] * behind_block[b]
        run = states[b] + block_decay * run
    m1[0, 16:32] = run

    for i in range(4):
        for j in range(4):
            mid[BL * j : BL * (j + 1), CD * i : CD * (i + 1)] = x[(4 * j + i) * BL : (4 * j + i + 1) * BL, :]
    part = nn(mid[...], swap[0]).astype(BF16)
    for i in range(4):
        for j in range(4):
            mid[BL * i : BL * (i + 1), CD * j : CD * (j + 1)] = part[BL * j : BL * (j + 1), CD * i : CD * (i + 1)]
    part = nn(mid[...], swap[1]).astype(BF16)
    for i in range(4):
        for j in range(4):
            xn[4 * j + i] = part[BL * i : BL * (i + 1), CD * j : CD * (j + 1)]
    regroup(y, yn, 32)

    pl.semaphore_wait(barrier, len(everyone))
    c_m1 = send(m1, quad_peers, 0)
    load_r.wait()
    load_k.wait()

    row_c, lane_c = iota((BL, BL), 0), iota((BL, BL), 1)
    flip = jnp.where(lane_c + row_c == BL - 1, 1.0, 0.0).astype(BF16)
    for g in range(NG):
        gram = nt(nn(flip, xn[g]).astype(BF16), yn[g])
        gram = pltpu.roll(gram, 1, 1, stride=1, stride_axis=0)
        lags[g : g + 1, :] = jnp.sum(jnp.where(lane_c <= row_c, gram, 0.0), axis=0, keepdims=True)

    h = cross
    for g in range(NG):
        terms = pw[MODES * g : MODES * (g + 1), :] * lags[g : g + 1, :]
        column = jnp.sum(terms, axis=1, keepdims=True)
        h = h + jnp.where(iota((MODES, CD), 1) == g, column, 0.0)
    skip_sum = jnp.zeros((BL, CD), F32)
    for b in range(NB):
        rows = slice(b * BL, (b + 1) * BL)
        skip_sum = skip_sum + x[rows, :].astype(F32) * y[rows, :].astype(F32)
    skip_sum = jnp.sum(skip_sum, axis=0, keepdims=True)
    gz[0] = pack(h) + jnp.where(iota((8, CD), 0) == 2, skip_sum, 0.0)
    c_gz = send(gz, z_peers, 1)

    dev = jnp.exp(-(float(TOK) * rmc))
    quad = jnp.exp(-(float(TOK * NQ) * rmc))
    slab = jnp.exp(-(float(TOK * NQ * NZ) * rmc))
    arrive(c_m1)
    load1 = lambda lo: lambda i: m1[lax.rem(i - q + NQ, NQ), lo : lo + 16]
    m2[0, 0:16] = suffix(load1(0), NQ, dev)
    p1, tq = pairs(load1(0), load1(16), NQ, dev)
    m2[0, 16:32] = tq
    m2[0, 32:40] = pack(p1)
    c_m2 = send(m2, z_peers, 2)

    twice = 2.0 * rates
    series = twice * (1.0 - twice / 2 * (1.0 - twice / 3 * (1.0 - twice / 4 * (
        1.0 - twice / 5 * (1.0 - twice / 6 * (1.0 - twice / 7 * (1.0 - twice / 8)))))))
    norm = jnp.sqrt(jnp.where(twice < 0.25, series, 1.0 - jnp.exp(-twice)))
    coef = res_ref[...] * norm
    for k in range(CD // NG):
        tmp[NG * k : NG * (k + 1), 0:MODES] = coef
    cmc_ref[...] = jnp.transpose(tmp[...])[:MODES]

    third = iota((BL, 3 * MODES), 1) // MODES
    left = (BL - iota((BL, 3 * MODES), 0)).astype(F32)

    def local_one(g):
        gs = slice(MODES * g, MODES * (g + 1))
        yq = yn[g]
        column = jnp.broadcast_to(cmc_ref[:, g : g + 1], (MODES, CD))
        taps = jnp.sum(column * pw[gs, :], axis=0, keepdims=True)
        toep = pltpu.roll(jnp.broadcast_to(taps, (BL, BL)), 0, 1, stride=1, stride_axis=0)
        th, tl = split(jnp.where(lane_c >= row_c, toep, 0.0))
        ah, al = split(column * after[gs, :])
        reach = jnp.exp(-(left * rates3[g : g + 1, :]))
        rh = reach.astype(BF16).astype(F32)
        reach = jnp.where(third == 1, reach - rh, rh).astype(BF16)
        on[g] = nn(
            jnp.concatenate([th, tl], axis=1), jnp.concatenate([yq, yq], axis=0)
        ) + nn(reach, jnp.concatenate([ah, ah, al], axis=0))

    for g, piece in enumerate(exchange([ab[b] for b in range(NB)])):
        after[MODES * g : MODES * (g + 1), :] = piece
    for g in range(NG):
        local_one(g)

    skip_row = skip_ref[...].reshape(1, CD)
    for r in range(0, BL, 16):
        for b, piece in enumerate(exchange([on[g, r : r + 16, :] for g in range(NG)])):
            rows = slice(b * BL + r, b * BL + r + 16)
            loc[rows, :] = piece + skip_row * y[rows, :].astype(F32)

    def add_up(buf, count):
        total = buf[0]
        for k in range(1, count):
            total = total + buf[k]
        return total

    arrive(c_gz)
    gq[0] = add_up(gz, NZ)
    c_gq = send(gq, quad_peers, 3)

    hl = TOK // 2
    column = jnp.concatenate(
        [jnp.broadcast_to(rmc[:, g : g + 1], (MODES, CD)) for g in range(NG)], axis=0
    )
    rowr = jnp.transpose(column)[0:1]
    for b in range(hl // BL):
        rows = slice(b * BL, (b + 1) * BL)
        away = (hl - b * BL - iota((BL, NG * MODES), 0)).astype(F32)
        qh[rows, :], ql[rows, :] = split(jnp.exp(-(away * rowr)))

    arrive(c_gq)
    lag_part = add_up(gq, NQ)
    arrive(c_m2)
    load2 = lambda lo: lambda i: m2[lax.rem(i - z + NZ, NZ), lo : lo + 16]
    m3[0, 0:16] = suffix(load2(0), NZ, quad)
    p2, ty = pairs(load2(0), load2(16), NZ, quad)
    m3[0, 16:32] = ty
    lag_part = lag_part + pack(p2)
    for k in range(NZ):
        lag_part = lag_part + m2[k, 32:40]
    m3[0, 32:40] = lag_part
    c_o3 = send(m3, o_peers, 4)
    c_m3 = send(m3, y_peers, 5)

    arrive(c_m3)
    one = jnp.ones((MODES, CD), F32)
    zero = jnp.zeros((MODES, CD), F32)
    inc_y, w = zero, one
    for k in range(1, NY):
        inc_y = inc_y + jnp.where(yy + k < NY, w, zero) * m3[k, 0:16]
        w = w * slab
    inc_z, w = zero, one
    for k in range(1, NZ):
        inc_z = inc_z + jnp.where(z + k < NZ, w, zero) * m2[k, 0:16]
        w = w * quad
    inc_q, w = zero, one
    for k in range(1, NQ):
        inc_q = inc_q + jnp.where(q + k < NQ, w, zero) * m1[k, 0:16]
        w = w * dev
    to_slab = jnp.exp(-(((NZ - 1 - z) * (TOK * NQ)).astype(F32) * rmc))
    to_quad = jnp.exp(-(((NQ - 1 - q) * TOK).astype(F32) * rmc))
    inc = inc_q + to_quad * (inc_z + to_slab * inc_y)

    late = cmc_ref[...] * inc
    early = late * half_decay
    group_of = iota((MODES, CD), 1) % NG

    def spread(v):
        return jnp.concatenate([jnp.where(group_of == g, v, 0.0) for g in range(NG)], axis=0)

    def both(v, u):
        return jnp.concatenate([spread(v), spread(u)], axis=1).astype(BF16)

    eh = early.astype(BF16).astype(F32)
    lh = late.astype(BF16).astype(F32)
    a_hi = both(eh, lh)
    a_lo = both(early - eh, late - lh)
    arrived = jnp.concatenate([a_hi, a_lo, a_hi], axis=0)
    step = 2 * BL
    for r in range(0, hl, step):
        rows, rows2 = slice(r, r + step), slice(hl + r, hl + r + step)
        hi, lo = qh[rows, :], ql[rows, :]
        add = nn(jnp.concatenate([hi, hi, lo], axis=1), arrived)
        outb[rows, :] = (loc[rows, :] + add[:, :CD]).astype(BF16)
        outb[rows2, :] = (loc[rows2, :] + add[:, CD:]).astype(BF16)

    for copy in sent[:-2]:
        copy.wait()
    total_len = TOK * NQ * NZ * NY
    load3 = lambda lo, base: lambda i: m3[base + lax.rem(i - yy + NY, NY), lo : lo + 16]
    p3, _ = pairs(load3(0, 0), load3(16, 0), NY, slab)
    base = m3[0, 32:40] + m3[1, 32:40] + m3[2, 32:40] + m3[3, 32:40]
    sg_ref[...] = (base[2:3] * (1.0 / math.sqrt(total_len))).reshape(CD)
    arrive(c_o3)
    p4, _ = pairs(load3(0, NY), load3(16, NY), NY, slab)
    base = base + m3[4, 32:40] + m3[5, 32:40] + m3[6, 32:40] + m3[7, 32:40]
    grads = fold(unpack(base) + p3 + p4)
    tmp[...] = jnp.zeros_like(tmp)
    tmp[0:MODES, :] = grads
    turned = jnp.transpose(tmp[...])[0:NG, 0:MODES]
    rg_ref[...] = turned * norm * (1.0 / math.sqrt(GROUP * total_len))

    for copy in sent[-2:]:
        copy.wait()


def deliver(a, b, c, to_a, to_b, to_c, sems):
    copies = [
        pltpu.make_async_copy(src, dst, sems.at[i])
        for i, (src, dst) in enumerate(((a, to_a), (b, to_b), (c, to_c)))
    ]
    for copy in copies:
        copy.start()
    for copy in copies:
        copy.wait()


def shards(inputs, cotangent, residues, decay_rates, skip_weight):
    vmem = pl.BlockSpec(memory_space=pltpu.VMEM)
    hbm = pl.BlockSpec(memory_space=pltpu.HBM)
    near = pl.pallas_call(
        kernel,
        out_shape=(
            pltpu.VMEM((TOK, CD), BF16),
            pltpu.VMEM((NG, MODES), F32),
            pltpu.VMEM((CD,), F32),
        ),
        in_specs=[hbm] * 5,
        out_specs=(vmem, vmem, vmem),
        scratch_shapes=[
            pltpu.VMEM((TOK, CD), BF16),
            pltpu.VMEM((TOK, CD), BF16),
            pltpu.VMEM((NG, MODES), F32),
            pltpu.VMEM((NG, MODES), F32),
            pltpu.VMEM((CD,), F32),
            pltpu.VMEM((NG, BL, CD), BF16),
            pltpu.VMEM((NG, BL, CD), BF16),
            pltpu.VMEM((CD, CD), F32),
            pltpu.VMEM((MODES, CD), F32),
            pltpu.VMEM((NG, 3 * MODES), F32),
            pltpu.VMEM((NG * MODES, BL), F32),
            pltpu.VMEM((NG * MODES, BL), F32),
            pltpu.VMEM((NG, BL), F32),
            pltpu.VMEM((NB, MODES, CD), F32),
            pltpu.VMEM((NG * MODES, CD), F32),
            pltpu.VMEM((NG, BL, CD), F32),
            pltpu.VMEM((4 * BL, 4 * CD), BF16),
            pltpu.VMEM((2, 4 * CD, 4 * CD), BF16),
            pltpu.VMEM((TOK, CD), F32),
            pltpu.VMEM((TOK // 2, NG * MODES), BF16),
            pltpu.VMEM((TOK // 2, NG * MODES), BF16),
            pltpu.VMEM((NQ, 32, CD), F32),
            pltpu.VMEM((NZ, 40, CD), F32),
            pltpu.VMEM((2 * NY, 40, CD), F32),
            pltpu.VMEM((NZ, 8, CD), F32),
            pltpu.VMEM((NQ, 8, CD), F32),
            pltpu.SemaphoreType.DMA((5,)),
            pltpu.SemaphoreType.DMA((6,)),
            pltpu.SemaphoreType.DMA((6,)),
        ],
        compiler_params=pltpu.CompilerParams(
            collective_id=0, has_side_effects=True, vmem_limit_bytes=32 << 20
        ),
    )(*[pltpu.with_memory_space_constraint(v, pltpu.HBM) for v in (inputs, cotangent, residues, decay_rates, skip_weight)])
    return pl.pallas_call(
        deliver,
        out_shape=(
            jax.ShapeDtypeStruct((TOK, CD), BF16),
            jax.ShapeDtypeStruct((NG, MODES), F32),
            jax.ShapeDtypeStruct((CD,), F32),
        ),
        in_specs=[vmem, vmem, vmem],
        out_specs=(hbm, hbm, hbm),
        scratch_shapes=[pltpu.SemaphoreType.DMA((3,))],
    )(*[pltpu.with_memory_space_constraint(v, pltpu.VMEM) for v in near])


def solution(mesh):
    placed = (P("seq", "chan"), P("seq", "chan"), P(), P(), P("chan"))
    return jax.shard_map(
        shards,
        mesh=mesh,
        in_specs=placed,
        out_specs=(P("seq", "chan"), P(), P("chan")),
        check_vma=False,
    )
```

```python
import math

import jax
import jax.numpy as jnp
from jax import lax
from jax.experimental import pallas as pl
from jax.experimental.pallas import tpu as pltpu
from jax.sharding import PartitionSpec as P

MESH = pl.DeviceIdType.MESH
F32 = jnp.float32
BF16 = jnp.bfloat16
NG = 16
MODES = 16
GROUP = 16
TOK = 2048
CD = 128
BL = 128
NB = TOK // BL
NQ, NZ, NY = 4, 8, 4


def split(v):
    hi = v.astype(BF16)
    return hi, (v - hi.astype(F32)).astype(BF16)


def nn(a, b):
    return lax.dot_general(a, b, (((1,), (0,)), ((), ())), preferred_element_type=F32)


def nt(a, b):
    return lax.dot_general(a, b, (((1,), (1,)), ((), ())), preferred_element_type=F32)


def iota(shape, dim):
    return lax.broadcasted_iota(jnp.int32, shape, dim)


def fold(h):
    h = h + pltpu.roll(h, 64, 1)
    h = h + pltpu.roll(h, 32, 1)
    return h + pltpu.roll(h, 16, 1)


def pack(h):
    h = fold(h)
    keep = iota((8, CD), 1) // 16 == iota((8, CD), 0)
    first = jnp.sum(jnp.where(keep, h[:8], 0.0), axis=0, keepdims=True)
    second = jnp.sum(jnp.where(keep, h[8:], 0.0), axis=0, keepdims=True)
    row = iota((8, CD), 0)
    return jnp.where(row == 0, first, jnp.where(row == 1, second, 0.0))


def unpack(tile):
    keep = iota((8, CD), 1) // 16 == iota((8, CD), 0)
    return jnp.concatenate(
        [jnp.where(keep, tile[0:1], 0.0), jnp.where(keep, tile[1:2], 0.0)], axis=0
    )


def extract(full):
    group_of = iota((MODES, CD), 1) % NG
    out = jnp.zeros((MODES, CD), F32)
    for g in range(NG):
        out = jnp.where(group_of == g, full[MODES * g : MODES * (g + 1)], out)
    return out


def swap_dot(bits):
    row, lane = iota((CD, CD), 0), iota((CD, CD), 1)
    same = ((row ^ lane) & ~(3 << bits)) == 0
    row_bits, lane_bits = (row >> bits) & 3, (lane >> bits) & 3
    return jnp.concatenate(
        [
            jnp.concatenate(
                [
                    jnp.where(same & (lane_bits == i) & (row_bits == j), 1.0, 0.0).astype(BF16)
                    for j in range(4)
                ],
                axis=1,
            )
            for i in range(4)
        ],
        axis=0,
    )


def suffix(load_s, count, w):
    acc = load_s(count - 1)
    for i in range(count - 2, -1, -1):
        acc = load_s(i) + w * acc
    return acc


def pairs(load_s, load_t, count, w):
    acc = load_t(0)
    total = None
    for i in range(1, count):
        term = acc * load_s(i)
        total = term if total is None else total + term
        acc = load_t(i) + w * acc
    return total, acc


def exchange(blocks):
    bit_of = iota(blocks[0].shape, 1)
    for k in (1, 2, 4, 8):
        keep = (bit_of & k) == 0
        for i in range(NG):
            if not i & k:
                low, high = blocks[i], blocks[i | k]
                blocks[i] = jnp.where(keep, low, pltpu.roll(high, k, 1))
                blocks[i | k] = jnp.where(keep, pltpu.roll(low, CD - k, 1), high)
    return blocks


def kernel(
    x_hbm, y_hbm, res_hbm, dec_hbm, skip_hbm,
    outb, rg_ref, sg_ref,
    x, y, res_ref, dec_ref, skip_ref, xn, yn, tmp, cmc_ref, rates3, pw, pt, lags, ab, after, on, mid, swap, loc, qh, ql,
    m1, m2, m3, gz, gq,
    load_sem, send_sem, recv_sem,
):
    me = lax.axis_index("seq")
    half = lax.axis_index("chan")
    q = lax.rem(me, NQ)
    z = lax.rem(me // NQ, NZ)
    yy = me // (NQ * NZ)

    def at(y_i, z_i, q_i, h_i):
        return {"seq": (y_i * NZ + z_i) * NQ + q_i, "chan": h_i}

    quad_peers = [(k, at(yy, z, lax.rem(q + NQ - k, NQ), half)) for k in (2, 3, 1)]
    z_peers = [(k, at(yy, lax.rem(z + NZ - k, NZ), q, half)) for k in (4, 3, 5, 2, 6, 1, 7)]
    y_peers = [(k, at(lax.rem(yy + NY - k, NY), z, q, half)) for k in (2, 1, 3)]
    o_peers = [(NY + k, at(lax.rem(yy + NY - k, NY), z, q, 1 - half)) for k in (2, 1, 3, 0)]

    load_y = pltpu.make_async_copy(y_hbm, y, load_sem.at[0])
    load_x = pltpu.make_async_copy(x_hbm, x, load_sem.at[1])
    load_r = pltpu.make_async_copy(res_hbm, res_ref, load_sem.at[2])
    load_d = pltpu.make_async_copy(dec_hbm, dec_ref, load_sem.at[3])
    load_k = pltpu.make_async_copy(skip_hbm, skip_ref, load_sem.at[4])
    load_d.start()
    load_y.start()
    load_x.start()
    barrier = pltpu.get_barrier_semaphore()
    everyone = z_peers + o_peers + y_peers + quad_peers
    for _, peer in everyone:
        pl.semaphore_signal(barrier, inc=1, device_id=peer, device_id_type=MESH)

    load_r.start()
    load_k.start()
    sent = []

    def send(buf, peers, sem):
        for slot, peer in peers:
            pltpu.make_async_remote_copy(
                src_ref=buf.at[0],
                dst_ref=buf.at[slot],
                send_sem=send_sem.at[sem],
                recv_sem=recv_sem.at[sem],
                device_id=peer,
                device_id_type=MESH,
            ).start()
        slots = [slot for slot, _ in peers]
        area = buf.at[min(slots) : max(slots) + 1]
        sent.append(pltpu.make_async_copy(area, area, send_sem.at[sem]))
        return pltpu.make_async_copy(area, area, recv_sem.at[sem])

    def arrive(copies):
        copies.wait()

    swap[0] = swap_dot(0)
    swap[1] = swap_dot(2)
    load_d.wait()
    rates = dec_ref[...]
    tmp[...] = jnp.zeros_like(tmp)
    for k in range(CD // NG):
        tmp[NG * k : NG * (k + 1), 0:MODES] = rates
    rmc = jnp.transpose(tmp[...])[:MODES]
    for k in range(3):
        rates3[:, MODES * k : MODES * (k + 1)] = rates
    ahead = iota((MODES, BL), 1).astype(F32)
    behind = BL - ahead
    for g in range(NG):
        column = jnp.broadcast_to(rmc[:, g : g + 1], (MODES, BL))
        pw[MODES * g : MODES * (g + 1), :] = jnp.exp(-(column * ahead))
        pt[MODES * g : MODES * (g + 1), :] = jnp.exp(-(column * behind))

    def regroup(src, dst, step):
        for r in range(0, BL, step):
            for g, piece in enumerate(exchange([src[b * BL + r : b * BL + r + step, :] for b in range(NB)])):
                dst[g, r : r + step, :] = piece

    block_decay = jnp.exp(-(float(BL) * rmc))
    half_decay = jnp.exp(-(float(TOK // 2) * rmc))

    row_c, lane_c = iota((BL, BL), 0), iota((BL, BL), 1)
    flip = jnp.where(lane_c + row_c == BL - 1, 1.0, 0.0).astype(BF16)

    def block_states(ref, powers, flipped=None):
        hi, lo = split(powers[...])
        rates_side = jnp.concatenate([hi, lo], axis=1)
        if flipped is not None:
            flip_side = jnp.concatenate([flip, jnp.zeros_like(flip)], axis=1)
            rates_side = jnp.concatenate([rates_side, flip_side], axis=0)
        states = []
        for b in range(0, NB, 2):
            two = jnp.concatenate(
                [ref[b * BL : (b + 1) * BL, :], ref[(b + 1) * BL : (b + 2) * BL, :]], axis=1
            )
            full = nn(rates_side, jnp.concatenate([two, two], axis=0))
            states += [extract(full[:, :CD]), extract(full[:, CD:])]
            if flipped is not None:
                j, i = b // 4, b % 4
                flipped[BL * j : BL * (j + 1), CD * i : CD * (i + 2)] = full[NG * MODES :].astype(BF16)
        return states

    load_y.wait()
    run = jnp.zeros((MODES, CD), F32)
    behind_block = [None] * NB
    states = block_states(y, pw)
    for b in range(NB - 1, -1, -1):
        behind_block[b] = run
        ab[b] = run
        run = states[b] + block_decay * run
    m1[0, 0:16] = run
    load_x.wait()
    states = block_states(x, pt, mid)
    run = states[0]
    cross = run * behind_block[0]
    for b in range(1, NB):
        cross = cross + states[b] * behind_block[b]
        run = states[b] + block_decay * run
    m1[0, 16:32] = run

    part = nn(mid[...], swap[0]).astype(BF16)
    for i in range(4):
        for j in range(4):
            mid[BL * i : BL * (i + 1), CD * j : CD * (j + 1)] = part[BL * j : BL * (j + 1), CD * i : CD * (i + 1)]
    part = nn(mid[...], swap[1]).astype(BF16)
    for i in range(4):
        for j in range(4):
            xn[4 * j + i] = part[BL * i : BL * (i + 1), CD * j : CD * (j + 1)]
    regroup(y, yn, 32)

    pl.semaphore_wait(barrier, len(everyone))
    c_m1 = send(m1, quad_peers, 0)
    load_r.wait()
    load_k.wait()

    for g in range(NG):
        gram = nt(xn[g], yn[g])
        gram = pltpu.roll(gram, 1, 1, stride=1, stride_axis=0)
        lags[g : g + 1, :] = jnp.sum(jnp.where(lane_c <= row_c, gram, 0.0), axis=0, keepdims=True)

    h = cross
    for g in range(NG):
        terms = pw[MODES * g : MODES * (g + 1), :] * lags[g : g + 1, :]
        column = jnp.sum(terms, axis=1, keepdims=True)
        h = h + jnp.where(iota((MODES, CD), 1) == g, column, 0.0)
    skip_sum = jnp.zeros((BL, CD), F32)
    for b in range(NB):
        rows = slice(b * BL, (b + 1) * BL)
        skip_sum = skip_sum + x[rows, :].astype(F32) * y[rows, :].astype(F32)
    skip_sum = jnp.sum(skip_sum, axis=0, keepdims=True)
    gz[0] = pack(h) + jnp.where(iota((8, CD), 0) == 2, skip_sum, 0.0)
    c_gz = send(gz, z_peers, 1)

    dev = jnp.exp(-(float(TOK) * rmc))
    quad = jnp.exp(-(float(TOK * NQ) * rmc))
    slab = jnp.exp(-(float(TOK * NQ * NZ) * rmc))
    arrive(c_m1)
    load1 = lambda lo: lambda i: m1[lax.rem(i - q + NQ, NQ), lo : lo + 16]
    m2[0, 0:16] = suffix(load1(0), NQ, dev)
    p1, tq = pairs(load1(0), load1(16), NQ, dev)
    m2[0, 16:32] = tq
    m2[0, 32:40] = pack(p1)
    c_m2 = send(m2, z_peers, 2)

    twice = 2.0 * rates
    series = twice * (1.0 - twice / 2 * (1.0 - twice / 3 * (1.0 - twice / 4 * (
        1.0 - twice / 5 * (1.0 - twice / 6 * (1.0 - twice / 7 * (1.0 - twice / 8)))))))
    norm = jnp.sqrt(jnp.where(twice < 0.25, series, 1.0 - jnp.exp(-twice)))
    coef = res_ref[...] * norm
    for k in range(CD // NG):
        tmp[NG * k : NG * (k + 1), 0:MODES] = coef
    cmc_ref[...] = jnp.transpose(tmp[...])[:MODES]

    third = iota((BL, 3 * MODES), 1) // MODES
    left = (BL - iota((BL, 3 * MODES), 0)).astype(F32)

    def local_one(g):
        gs = slice(MODES * g, MODES * (g + 1))
        yq = yn[g]
        column = jnp.broadcast_to(cmc_ref[:, g : g + 1], (MODES, CD))
        taps = jnp.sum(column * pw[gs, :], axis=0, keepdims=True)
        toep = pltpu.roll(jnp.broadcast_to(taps, (BL, BL)), 0, 1, stride=1, stride_axis=0)
        th, tl = split(jnp.where(lane_c >= row_c, toep, 0.0))
        ah, al = split(column * after[gs, :])
        reach = jnp.exp(-(left * rates3[g : g + 1, :]))
        rh = reach.astype(BF16).astype(F32)
        reach = jnp.where(third == 1, reach - rh, rh).astype(BF16)
        on[g] = nn(
            jnp.concatenate([th, tl], axis=1), jnp.concatenate([yq, yq], axis=0)
        ) + nn(reach, jnp.concatenate([ah, ah, al], axis=0))

    for g, piece in enumerate(exchange([ab[b] for b in range(NB)])):
        after[MODES * g : MODES * (g + 1), :] = piece
    for g in range(NG):
        local_one(g)

    skip_row = skip_ref[...].reshape(1, CD)
    for r in range(0, BL, 16):
        for b, piece in enumerate(exchange([on[g, r : r + 16, :] for g in range(NG)])):
            rows = slice(b * BL + r, b * BL + r + 16)
            loc[rows, :] = piece + skip_row * y[rows, :].astype(F32)

    def add_up(buf, count):
        total = buf[0]
        for k in range(1, count):
            total = total + buf[k]
        return total

    arrive(c_gz)
    gq[0] = add_up(gz, NZ)
    c_gq = send(gq, quad_peers, 3)

    hl = TOK // 2
    column = jnp.concatenate(
        [jnp.broadcast_to(rmc[:, g : g + 1], (MODES, CD)) for g in range(NG)], axis=0
    )
    rowr = jnp.transpose(column)[0:1]
    for b in range(hl // BL):
        rows = slice(b * BL, (b + 1) * BL)
        away = (hl - b * BL - iota((BL, NG * MODES), 0)).astype(F32)
        qh[rows, :], ql[rows, :] = split(jnp.exp(-(away * rowr)))

    arrive(c_gq)
    lag_part = add_up(gq, NQ)
    arrive(c_m2)
    load2 = lambda lo: lambda i: m2[lax.rem(i - z + NZ, NZ), lo : lo + 16]
    m3[0, 0:16] = suffix(load2(0), NZ, quad)
    p2, ty = pairs(load2(0), load2(16), NZ, quad)
    m3[0, 16:32] = ty
    lag_part = lag_part + pack(p2)
    for k in range(NZ):
        lag_part = lag_part + m2[k, 32:40]
    m3[0, 32:40] = lag_part
    c_o3 = send(m3, o_peers, 4)
    c_m3 = send(m3, y_peers, 5)

    arrive(c_m3)
    one = jnp.ones((MODES, CD), F32)
    zero = jnp.zeros((MODES, CD), F32)
    inc_y, w = zero, one
    for k in range(1, NY):
        inc_y = inc_y + jnp.where(yy + k < NY, w, zero) * m3[k, 0:16]
        w = w * slab
    inc_z, w = zero, one
    for k in range(1, NZ):
        inc_z = inc_z + jnp.where(z + k < NZ, w, zero) * m2[k, 0:16]
        w = w * quad
    inc_q, w = zero, one
    for k in range(1, NQ):
        inc_q = inc_q + jnp.where(q + k < NQ, w, zero) * m1[k, 0:16]
        w = w * dev
    to_slab = jnp.exp(-(((NZ - 1 - z) * (TOK * NQ)).astype(F32) * rmc))
    to_quad = jnp.exp(-(((NQ - 1 - q) * TOK).astype(F32) * rmc))
    inc = inc_q + to_quad * (inc_z + to_slab * inc_y)

    late = cmc_ref[...] * inc
    early = late * half_decay
    group_of = iota((MODES, CD), 1) % NG

    def spread(v):
        return jnp.concatenate([jnp.where(group_of == g, v, 0.0) for g in range(NG)], axis=0)

    def both(v, u):
        return jnp.concatenate([spread(v), spread(u)], axis=1).astype(BF16)

    eh = early.astype(BF16).astype(F32)
    lh = late.astype(BF16).astype(F32)
    a_hi = both(eh, lh)
    a_lo = both(early - eh, late - lh)
    arrived = jnp.concatenate([a_hi, a_lo, a_hi], axis=0)
    step = 2 * BL
    for r in range(0, hl, step):
        rows, rows2 = slice(r, r + step), slice(hl + r, hl + r + step)
        hi, lo = qh[rows, :], ql[rows, :]
        add = nn(jnp.concatenate([hi, hi, lo], axis=1), arrived)
        outb[rows, :] = (loc[rows, :] + add[:, :CD]).astype(BF16)
        outb[rows2, :] = (loc[rows2, :] + add[:, CD:]).astype(BF16)

    for copy in sent[:-2]:
        copy.wait()
    total_len = TOK * NQ * NZ * NY
    load3 = lambda lo, base: lambda i: m3[base + lax.rem(i - yy + NY, NY), lo : lo + 16]
    p3, _ = pairs(load3(0, 0), load3(16, 0), NY, slab)
    base = m3[0, 32:40] + m3[1, 32:40] + m3[2, 32:40] + m3[3, 32:40]
    sg_ref[...] = (base[2:3] * (1.0 / math.sqrt(total_len))).reshape(CD)
    arrive(c_o3)
    p4, _ = pairs(load3(0, NY), load3(16, NY), NY, slab)
    base = base + m3[4, 32:40] + m3[5, 32:40] + m3[6, 32:40] + m3[7, 32:40]
    grads = fold(unpack(base) + p3 + p4)
    tmp[...] = jnp.zeros_like(tmp)
    tmp[0:MODES, :] = grads
    turned = jnp.transpose(tmp[...])[0:NG, 0:MODES]
    rg_ref[...] = turned * norm * (1.0 / math.sqrt(GROUP * total_len))

    for copy in sent[-2:]:
        copy.wait()


def deliver(a, b, c, to_a, to_b, to_c, sems):
    copies = [
        pltpu.make_async_copy(src, dst, sems.at[i])
        for i, (src, dst) in enumerate(((a, to_a), (b, to_b), (c, to_c)))
    ]
    for copy in copies:
        copy.start()
    for copy in copies:
        copy.wait()


def shards(inputs, cotangent, residues, decay_rates, skip_weight):
    vmem = pl.BlockSpec(memory_space=pltpu.VMEM)
    hbm = pl.BlockSpec(memory_space=pltpu.HBM)
    near = pl.pallas_call(
        kernel,
        out_shape=(
            pltpu.VMEM((TOK, CD), BF16),
            pltpu.VMEM((NG, MODES), F32),
            pltpu.VMEM((CD,), F32),
        ),
        in_specs=[hbm] * 5,
        out_specs=(vmem, vmem, vmem),
        scratch_shapes=[
            pltpu.VMEM((TOK, CD), BF16),
            pltpu.VMEM((TOK, CD), BF16),
            pltpu.VMEM((NG, MODES), F32),
            pltpu.VMEM((NG, MODES), F32),
            pltpu.VMEM((CD,), F32),
            pltpu.VMEM((NG, BL, CD), BF16),
            pltpu.VMEM((NG, BL, CD), BF16),
            pltpu.VMEM((CD, CD), F32),
            pltpu.VMEM((MODES, CD), F32),
            pltpu.VMEM((NG, 3 * MODES), F32),
            pltpu.VMEM((NG * MODES, BL), F32),
            pltpu.VMEM((NG * MODES, BL), F32),
            pltpu.VMEM((NG, BL), F32),
            pltpu.VMEM((NB, MODES, CD), F32),
            pltpu.VMEM((NG * MODES, CD), F32),
            pltpu.VMEM((NG, BL, CD), F32),
            pltpu.VMEM((4 * BL, 4 * CD), BF16),
            pltpu.VMEM((2, 4 * CD, 4 * CD), BF16),
            pltpu.VMEM((TOK, CD), F32),
            pltpu.VMEM((TOK // 2, NG * MODES), BF16),
            pltpu.VMEM((TOK // 2, NG * MODES), BF16),
            pltpu.VMEM((NQ, 32, CD), F32),
            pltpu.VMEM((NZ, 40, CD), F32),
            pltpu.VMEM((2 * NY, 40, CD), F32),
            pltpu.VMEM((NZ, 8, CD), F32),
            pltpu.VMEM((NQ, 8, CD), F32),
            pltpu.SemaphoreType.DMA((5,)),
            pltpu.SemaphoreType.DMA((6,)),
            pltpu.SemaphoreType.DMA((6,)),
        ],
        compiler_params=pltpu.CompilerParams(
            collective_id=0, has_side_effects=True, vmem_limit_bytes=32 << 20
        ),
    )(*[pltpu.with_memory_space_constraint(v, pltpu.HBM) for v in (inputs, cotangent, residues, decay_rates, skip_weight)])
    return pl.pallas_call(
        deliver,
        out_shape=(
            jax.ShapeDtypeStruct((TOK, CD), BF16),
            jax.ShapeDtypeStruct((NG, MODES), F32),
            jax.ShapeDtypeStruct((CD,), F32),
        ),
        in_specs=[vmem, vmem, vmem],
        out_specs=(hbm, hbm, hbm),
        scratch_shapes=[pltpu.SemaphoreType.DMA((3,))],
    )(*[pltpu.with_memory_space_constraint(v, pltpu.VMEM) for v in near])


def solution(mesh):
    placed = (P("seq", "chan"), P("seq", "chan"), P(), P(), P("chan"))
    return jax.shard_map(
        shards,
        mesh=mesh,
        in_specs=placed,
        out_specs=(P("seq", "chan"), P(), P("chan")),
        check_vma=False,
    )
```

```python
import math

import jax
import jax.numpy as jnp
from jax import lax
from jax.experimental import pallas as pl
from jax.experimental.pallas import tpu as pltpu
from jax.sharding import PartitionSpec as P

MESH = pl.DeviceIdType.MESH
F32 = jnp.float32
BF16 = jnp.bfloat16
NG = 16
MODES = 16
GROUP = 16
TOK = 2048
CD = 128
BL = 128
NB = TOK // BL
NQ, NZ, NY = 4, 8, 4


def split(v):
    hi = v.astype(BF16)
    return hi, (v - hi.astype(F32)).astype(BF16)


def nn(a, b):
    return lax.dot_general(a, b, (((1,), (0,)), ((), ())), preferred_element_type=F32)


def nt(a, b):
    return lax.dot_general(a, b, (((1,), (1,)), ((), ())), preferred_element_type=F32)


def iota(shape, dim):
    return lax.broadcasted_iota(jnp.int32, shape, dim)


def fold(h):
    h = h + pltpu.roll(h, 64, 1)
    h = h + pltpu.roll(h, 32, 1)
    return h + pltpu.roll(h, 16, 1)


def pack(h):
    h = fold(h)
    keep = iota((8, CD), 1) // 16 == iota((8, CD), 0)
    first = jnp.sum(jnp.where(keep, h[:8], 0.0), axis=0, keepdims=True)
    second = jnp.sum(jnp.where(keep, h[8:], 0.0), axis=0, keepdims=True)
    row = iota((8, CD), 0)
    return jnp.where(row == 0, first, jnp.where(row == 1, second, 0.0))


def unpack(tile):
    keep = iota((8, CD), 1) // 16 == iota((8, CD), 0)
    return jnp.concatenate(
        [jnp.where(keep, tile[0:1], 0.0), jnp.where(keep, tile[1:2], 0.0)], axis=0
    )


def extract(full):
    group_of = iota((MODES, CD), 1) % NG
    out = jnp.zeros((MODES, CD), F32)
    for g in range(NG):
        out = jnp.where(group_of == g, full[MODES * g : MODES * (g + 1)], out)
    return out


def swap_dot(bits):
    row, lane = iota((CD, CD), 0), iota((CD, CD), 1)
    same = ((row ^ lane) & ~(3 << bits)) == 0
    row_bits, lane_bits = (row >> bits) & 3, (lane >> bits) & 3
    return jnp.concatenate(
        [
            jnp.concatenate(
                [
                    jnp.where(same & (lane_bits == i) & (row_bits == j), 1.0, 0.0).astype(BF16)
                    for j in range(4)
                ],
                axis=1,
            )
            for i in range(4)
        ],
        axis=0,
    )


def suffix(load_s, count, w):
    acc = load_s(count - 1)
    for i in range(count - 2, -1, -1):
        acc = load_s(i) + w * acc
    return acc


def pairs(load_s, load_t, count, w):
    acc = load_t(0)
    total = None
    for i in range(1, count):
        term = acc * load_s(i)
        total = term if total is None else total + term
        acc = load_t(i) + w * acc
    return total, acc


def exchange(blocks):
    bit_of = iota(blocks[0].shape, 1)
    for k in (1, 2, 4, 8):
        keep = (bit_of & k) == 0
        for i in range(NG):
            if not i & k:
                low, high = blocks[i], blocks[i | k]
                blocks[i] = jnp.where(keep, low, pltpu.roll(high, k, 1))
                blocks[i | k] = jnp.where(keep, pltpu.roll(low, CD - k, 1), high)
    return blocks


def kernel(
    x_hbm, y_hbm, res_hbm, dec_hbm, skip_hbm,
    outb, rg_ref, sg_ref,
    x, y, res_ref, dec_ref, skip_ref, xn, yn, tmp, cmc_ref, rates3, pw, pt, lags, ab, after, on, mid, swap, loc, qh, ql,
    m1, m2, m3, gz, gq,
    load_sem, send_sem, recv_sem,
):
    me = lax.axis_index("seq")
    half = lax.axis_index("chan")
    q = lax.rem(me, NQ)
    z = lax.rem(me // NQ, NZ)
    yy = me // (NQ * NZ)

    def at(y_i, z_i, q_i, h_i):
        return {"seq": (y_i * NZ + z_i) * NQ + q_i, "chan": h_i}

    quad_peers = [(k, at(yy, z, lax.rem(q + NQ - k, NQ), half)) for k in (2, 3, 1)]
    z_peers = [(k, at(yy, lax.rem(z + NZ - k, NZ), q, half)) for k in (4, 3, 5, 2, 6, 1, 7)]
    y_peers = [(k, at(lax.rem(yy + NY - k, NY), z, q, half)) for k in (2, 1, 3)]
    near = lax.rem(q + 2, NQ)
    o_peers = [(NY + k, at(lax.rem(yy + NY - k, NY), z, near, 1 - half)) for k in (2, 1, 3, 0)]

    load_y = pltpu.make_async_copy(y_hbm, y, load_sem.at[0])
    load_x = pltpu.make_async_copy(x_hbm, x, load_sem.at[1])
    load_r = pltpu.make_async_copy(res_hbm, res_ref, load_sem.at[2])
    load_d = pltpu.make_async_copy(dec_hbm, dec_ref, load_sem.at[3])
    load_k = pltpu.make_async_copy(skip_hbm, skip_ref, load_sem.at[4])
    load_d.start()
    load_y.start()
    load_x.start()
    barrier = pltpu.get_barrier_semaphore()
    everyone = z_peers + o_peers + y_peers + quad_peers
    for _, peer in everyone:
        pl.semaphore_signal(barrier, inc=1, device_id=peer, device_id_type=MESH)

    load_r.start()
    load_k.start()
    sent = []

    def send(buf, peers, sem):
        for slot, peer in peers:
            pltpu.make_async_remote_copy(
                src_ref=buf.at[0],
                dst_ref=buf.at[slot],
                send_sem=send_sem.at[sem],
                recv_sem=recv_sem.at[sem],
                device_id=peer,
                device_id_type=MESH,
            ).start()
        slots = [slot for slot, _ in peers]
        area = buf.at[min(slots) : max(slots) + 1]
        sent.append(pltpu.make_async_copy(area, area, send_sem.at[sem]))
        return pltpu.make_async_copy(area, area, recv_sem.at[sem])

    def arrive(copies):
        copies.wait()

    swap[0] = swap_dot(0)
    swap[1] = swap_dot(2)
    load_d.wait()
    rates = dec_ref[...]
    tmp[...] = jnp.zeros_like(tmp)
    for k in range(CD // NG):
        tmp[NG * k : NG * (k + 1), 0:MODES] = rates
    rmc = jnp.transpose(tmp[...])[:MODES]
    for k in range(3):
        rates3[:, MODES * k : MODES * (k + 1)] = rates
    ahead = iota((MODES, BL), 1).astype(F32)
    behind = BL - ahead
    for g in range(NG):
        column = jnp.broadcast_to(rmc[:, g : g + 1], (MODES, BL))
        pw[MODES * g : MODES * (g + 1), :] = jnp.exp(-(column * ahead))
        pt[MODES * g : MODES * (g + 1), :] = jnp.exp(-(column * behind))

    def regroup(src, dst, step):
        for r in range(0, BL, step):
            for g, piece in enumerate(exchange([src[b * BL + r : b * BL + r + step, :] for b in range(NB)])):
                dst[g, r : r + step, :] = piece

    block_decay = jnp.exp(-(float(BL) * rmc))
    half_decay = jnp.exp(-(float(TOK // 2) * rmc))

    row_c, lane_c = iota((BL, BL), 0), iota((BL, BL), 1)
    flip = jnp.where(lane_c + row_c == BL - 1, 1.0, 0.0).astype(BF16)

    def block_states(ref, powers, flipped=None):
        hi, lo = split(powers[...])
        rates_side = jnp.concatenate([hi, lo], axis=1)
        if flipped is not None:
            flip_side = jnp.concatenate([flip, jnp.zeros_like(flip)], axis=1)
            rates_side = jnp.concatenate([rates_side, flip_side], axis=0)
        states = []
        for b in range(0, NB, 2):
            two = jnp.concatenate(
                [ref[b * BL : (b + 1) * BL, :], ref[(b + 1) * BL : (b + 2) * BL, :]], axis=1
            )
            full = nn(rates_side, jnp.concatenate([two, two], axis=0))
            states += [extract(full[:, :CD]), extract(full[:, CD:])]
            if flipped is not None:
                j, i = b // 4, b % 4
                flipped[BL * j : BL * (j + 1), CD * i : CD * (i + 2)] = full[NG * MODES :].astype(BF16)
        return states

    load_y.wait()
    run = jnp.zeros((MODES, CD), F32)
    behind_block = [None] * NB
    states = block_states(y, pw)
    for b in range(NB - 1, -1, -1):
        behind_block[b] = run
        ab[b] = run
        run = states[b] + block_decay * run
    m1[0, 0:16] = run
    load_x.wait()
    states = block_states(x, pt, mid)
    run = states[0]
    cross = run * behind_block[0]
    for b in range(1, NB):
        cross = cross + states[b] * behind_block[b]
        run = states[b] + block_decay * run
    m1[0, 16:32] = run

    part = nn(mid[...], swap[0]).astype(BF16)
    for i in range(4):
        for j in range(4):
            mid[BL * i : BL * (i + 1), CD * j : CD * (j + 1)] = part[BL * j : BL * (j + 1), CD * i : CD * (i + 1)]
    part = nn(mid[...], swap[1]).astype(BF16)
    for i in range(4):
        for j in range(4):
            xn[4 * j + i] = part[BL * i : BL * (i + 1), CD * j : CD * (j + 1)]
    regroup(y, yn, 32)

    pl.semaphore_wait(barrier, len(everyone))
    c_m1 = send(m1, quad_peers, 0)
    load_r.wait()
    load_k.wait()

    for g in range(NG):
        gram = nt(xn[g], yn[g])
        gram = pltpu.roll(gram, 1, 1, stride=1, stride_axis=0)
        lags[g : g + 1, :] = jnp.sum(jnp.where(lane_c <= row_c, gram, 0.0), axis=0, keepdims=True)

    h = cross
    for g in range(NG):
        terms = pw[MODES * g : MODES * (g + 1), :] * lags[g : g + 1, :]
        column = jnp.sum(terms, axis=1, keepdims=True)
        h = h + jnp.where(iota((MODES, CD), 1) == g, column, 0.0)
    skip_sum = jnp.zeros((BL, CD), F32)
    for b in range(NB):
        rows = slice(b * BL, (b + 1) * BL)
        skip_sum = skip_sum + x[rows, :].astype(F32) * y[rows, :].astype(F32)
    skip_sum = jnp.sum(skip_sum, axis=0, keepdims=True)
    gz[0] = pack(h) + jnp.where(iota((8, CD), 0) == 2, skip_sum, 0.0)
    c_gz = send(gz, z_peers, 1)

    dev = jnp.exp(-(float(TOK) * rmc))
    quad = jnp.exp(-(float(TOK * NQ) * rmc))
    slab = jnp.exp(-(float(TOK * NQ * NZ) * rmc))
    arrive(c_m1)
    load1 = lambda lo: lambda i: m1[lax.rem(i - q + NQ, NQ), lo : lo + 16]
    m2[0, 0:16] = suffix(load1(0), NQ, dev)
    p1, tq = pairs(load1(0), load1(16), NQ, dev)
    m2[0, 16:32] = tq
    m2[0, 32:40] = pack(p1)
    c_m2 = send(m2, z_peers, 2)

    twice = 2.0 * rates
    series = twice * (1.0 - twice / 2 * (1.0 - twice / 3 * (1.0 - twice / 4 * (
        1.0 - twice / 5 * (1.0 - twice / 6 * (1.0 - twice / 7 * (1.0 - twice / 8)))))))
    norm = jnp.sqrt(jnp.where(twice < 0.25, series, 1.0 - jnp.exp(-twice)))
    coef = res_ref[...] * norm
    for k in range(CD // NG):
        tmp[NG * k : NG * (k + 1), 0:MODES] = coef
    cmc_ref[...] = jnp.transpose(tmp[...])[:MODES]

    third = iota((BL, 3 * MODES), 1) // MODES
    left = (BL - iota((BL, 3 * MODES), 0)).astype(F32)

    def local_one(g):
        gs = slice(MODES * g, MODES * (g + 1))
        yq = yn[g]
        column = jnp.broadcast_to(cmc_ref[:, g : g + 1], (MODES, CD))
        taps = jnp.sum(column * pw[gs, :], axis=0, keepdims=True)
        toep = pltpu.roll(jnp.broadcast_to(taps, (BL, BL)), 0, 1, stride=1, stride_axis=0)
        th, tl = split(jnp.where(lane_c >= row_c, toep, 0.0))
        ah, al = split(column * after[gs, :])
        reach = jnp.exp(-(left * rates3[g : g + 1, :]))
        rh = reach.astype(BF16).astype(F32)
        reach = jnp.where(third == 1, reach - rh, rh).astype(BF16)
        on[g] = nn(
            jnp.concatenate([th, tl], axis=1), jnp.concatenate([yq, yq], axis=0)
        ) + nn(reach, jnp.concatenate([ah, ah, al], axis=0))

    for g, piece in enumerate(exchange([ab[b] for b in range(NB)])):
        after[MODES * g : MODES * (g + 1), :] = piece
    for g in range(NG):
        local_one(g)

    skip_row = skip_ref[...].reshape(1, CD)
    for r in range(0, BL, 16):
        for b, piece in enumerate(exchange([on[g, r : r + 16, :] for g in range(NG)])):
            rows = slice(b * BL + r, b * BL + r + 16)
            loc[rows, :] = piece + skip_row * y[rows, :].astype(F32)

    def add_up(buf, count):
        total = buf[0]
        for k in range(1, count):
            total = total + buf[k]
        return total

    arrive(c_gz)
    gq[0] = add_up(gz, NZ)
    c_gq = send(gq, quad_peers, 3)

    hl = TOK // 2
    column = jnp.concatenate(
        [jnp.broadcast_to(rmc[:, g : g + 1], (MODES, CD)) for g in range(NG)], axis=0
    )
    rowr = jnp.transpose(column)[0:1]
    for b in range(hl // BL):
        rows = slice(b * BL, (b + 1) * BL)
        away = (hl - b * BL - iota((BL, NG * MODES), 0)).astype(F32)
        qh[rows, :], ql[rows, :] = split(jnp.exp(-(away * rowr)))

    arrive(c_gq)
    lag_part = add_up(gq, NQ)
    arrive(c_m2)
    load2 = lambda lo: lambda i: m2[lax.rem(i - z + NZ, NZ), lo : lo + 16]
    m3[0, 0:16] = suffix(load2(0), NZ, quad)
    p2, ty = pairs(load2(0), load2(16), NZ, quad)
    m3[0, 16:32] = ty
    lag_part = lag_part + pack(p2)
    for k in range(NZ):
        lag_part = lag_part + m2[k, 32:40]
    m3[0, 32:40] = lag_part
    c_o3 = send(m3, o_peers, 4)
    c_m3 = send(m3, y_peers, 5)

    arrive(c_m3)
    one = jnp.ones((MODES, CD), F32)
    zero = jnp.zeros((MODES, CD), F32)
    inc_y, w = zero, one
    for k in range(1, NY):
        inc_y = inc_y + jnp.where(yy + k < NY, w, zero) * m3[k, 0:16]
        w = w * slab
    inc_z, w = zero, one
    for k in range(1, NZ):
        inc_z = inc_z + jnp.where(z + k < NZ, w, zero) * m2[k, 0:16]
        w = w * quad
    inc_q, w = zero, one
    for k in range(1, NQ):
        inc_q = inc_q + jnp.where(q + k < NQ, w, zero) * m1[k, 0:16]
        w = w * dev
    to_slab = jnp.exp(-(((NZ - 1 - z) * (TOK * NQ)).astype(F32) * rmc))
    to_quad = jnp.exp(-(((NQ - 1 - q) * TOK).astype(F32) * rmc))
    inc = inc_q + to_quad * (inc_z + to_slab * inc_y)

    late = cmc_ref[...] * inc
    early = late * half_decay
    group_of = iota((MODES, CD), 1) % NG

    def spread(v):
        return jnp.concatenate([jnp.where(group_of == g, v, 0.0) for g in range(NG)], axis=0)

    def both(v, u):
        return jnp.concatenate([spread(v), spread(u)], axis=1).astype(BF16)

    eh = early.astype(BF16).astype(F32)
    lh = late.astype(BF16).astype(F32)
    a_hi = both(eh, lh)
    a_lo = both(early - eh, late - lh)
    arrived = jnp.concatenate([a_hi, a_lo, a_hi], axis=0)
    step = 2 * BL
    for r in range(0, hl, step):
        rows, rows2 = slice(r, r + step), slice(hl + r, hl + r + step)
        hi, lo = qh[rows, :], ql[rows, :]
        add = nn(jnp.concatenate([hi, hi, lo], axis=1), arrived)
        outb[rows, :] = (loc[rows, :] + add[:, :CD]).astype(BF16)
        outb[rows2, :] = (loc[rows2, :] + add[:, CD:]).astype(BF16)

    for copy in sent[:-2]:
        copy.wait()
    total_len = TOK * NQ * NZ * NY
    load3 = lambda lo, base: lambda i: m3[base + lax.rem(i - yy + NY, NY), lo : lo + 16]
    p3, _ = pairs(load3(0, 0), load3(16, 0), NY, slab)
    base = m3[0, 32:40] + m3[1, 32:40] + m3[2, 32:40] + m3[3, 32:40]
    sg_ref[...] = (base[2:3] * (1.0 / math.sqrt(total_len))).reshape(CD)
    arrive(c_o3)
    p4, _ = pairs(load3(0, NY), load3(16, NY), NY, slab)
    base = base + m3[4, 32:40] + m3[5, 32:40] + m3[6, 32:40] + m3[7, 32:40]
    grads = fold(unpack(base) + p3 + p4)
    tmp[...] = jnp.zeros_like(tmp)
    tmp[0:MODES, :] = grads
    turned = jnp.transpose(tmp[...])[0:NG, 0:MODES]
    rg_ref[...] = turned * norm * (1.0 / math.sqrt(GROUP * total_len))

    for copy in sent[-2:]:
        copy.wait()


def deliver(a, b, c, to_a, to_b, to_c, sems):
    copies = [
        pltpu.make_async_copy(src, dst, sems.at[i])
        for i, (src, dst) in enumerate(((a, to_a), (b, to_b), (c, to_c)))
    ]
    for copy in copies:
        copy.start()
    for copy in copies:
        copy.wait()


def shards(inputs, cotangent, residues, decay_rates, skip_weight):
    vmem = pl.BlockSpec(memory_space=pltpu.VMEM)
    hbm = pl.BlockSpec(memory_space=pltpu.HBM)
    near = pl.pallas_call(
        kernel,
        out_shape=(
            pltpu.VMEM((TOK, CD), BF16),
            pltpu.VMEM((NG, MODES), F32),
            pltpu.VMEM((CD,), F32),
        ),
        in_specs=[hbm] * 5,
        out_specs=(vmem, vmem, vmem),
        scratch_shapes=[
            pltpu.VMEM((TOK, CD), BF16),
            pltpu.VMEM((TOK, CD), BF16),
            pltpu.VMEM((NG, MODES), F32),
            pltpu.VMEM((NG, MODES), F32),
            pltpu.VMEM((CD,), F32),
            pltpu.VMEM((NG, BL, CD), BF16),
            pltpu.VMEM((NG, BL, CD), BF16),
            pltpu.VMEM((CD, CD), F32),
            pltpu.VMEM((MODES, CD), F32),
            pltpu.VMEM((NG, 3 * MODES), F32),
            pltpu.VMEM((NG * MODES, BL), F32),
            pltpu.VMEM((NG * MODES, BL), F32),
            pltpu.VMEM((NG, BL), F32),
            pltpu.VMEM((NB, MODES, CD), F32),
            pltpu.VMEM((NG * MODES, CD), F32),
            pltpu.VMEM((NG, BL, CD), F32),
            pltpu.VMEM((4 * BL, 4 * CD), BF16),
            pltpu.VMEM((2, 4 * CD, 4 * CD), BF16),
            pltpu.VMEM((TOK, CD), F32),
            pltpu.VMEM((TOK // 2, NG * MODES), BF16),
            pltpu.VMEM((TOK // 2, NG * MODES), BF16),
            pltpu.VMEM((NQ, 32, CD), F32),
            pltpu.VMEM((NZ, 40, CD), F32),
            pltpu.VMEM((2 * NY, 40, CD), F32),
            pltpu.VMEM((NZ, 8, CD), F32),
            pltpu.VMEM((NQ, 8, CD), F32),
            pltpu.SemaphoreType.DMA((5,)),
            pltpu.SemaphoreType.DMA((6,)),
            pltpu.SemaphoreType.DMA((6,)),
        ],
        compiler_params=pltpu.CompilerParams(
            collective_id=0, has_side_effects=True, vmem_limit_bytes=32 << 20
        ),
    )(*[pltpu.with_memory_space_constraint(v, pltpu.HBM) for v in (inputs, cotangent, residues, decay_rates, skip_weight)])
    return pl.pallas_call(
        deliver,
        out_shape=(
            jax.ShapeDtypeStruct((TOK, CD), BF16),
            jax.ShapeDtypeStruct((NG, MODES), F32),
            jax.ShapeDtypeStruct((CD,), F32),
        ),
        in_specs=[vmem, vmem, vmem],
        out_specs=(hbm, hbm, hbm),
        scratch_shapes=[pltpu.SemaphoreType.DMA((3,))],
    )(*[pltpu.with_memory_space_constraint(v, pltpu.VMEM) for v in near])


def solution(mesh):
    placed = (P("seq", "chan"), P("seq", "chan"), P(), P(), P("chan"))
    return jax.shard_map(
        shards,
        mesh=mesh,
        in_specs=placed,
        out_specs=(P("seq", "chan"), P(), P("chan")),
        check_vma=False,
    )
```

```python
import math

import jax
import jax.numpy as jnp
from jax import lax
from jax.experimental import pallas as pl
from jax.experimental.pallas import tpu as pltpu
from jax.sharding import PartitionSpec as P

MESH = pl.DeviceIdType.MESH
F32 = jnp.float32
BF16 = jnp.bfloat16
NG = 16
MODES = 16
GROUP = 16
TOK = 2048
CD = 128
BL = 128
NB = TOK // BL
NQ, NZ, NY = 4, 8, 4


def split(v):
    hi = v.astype(BF16)
    return hi, (v - hi.astype(F32)).astype(BF16)


def nn(a, b):
    return lax.dot_general(a, b, (((1,), (0,)), ((), ())), preferred_element_type=F32)


def nt(a, b):
    return lax.dot_general(a, b, (((1,), (1,)), ((), ())), preferred_element_type=F32)


def iota(shape, dim):
    return lax.broadcasted_iota(jnp.int32, shape, dim)


def fold(h):
    h = h + pltpu.roll(h, 64, 1)
    h = h + pltpu.roll(h, 32, 1)
    return h + pltpu.roll(h, 16, 1)


def pack(h):
    h = fold(h)
    keep = iota((8, CD), 1) // 16 == iota((8, CD), 0)
    first = jnp.sum(jnp.where(keep, h[:8], 0.0), axis=0, keepdims=True)
    second = jnp.sum(jnp.where(keep, h[8:], 0.0), axis=0, keepdims=True)
    row = iota((8, CD), 0)
    return jnp.where(row == 0, first, jnp.where(row == 1, second, 0.0))


def unpack(tile):
    keep = iota((8, CD), 1) // 16 == iota((8, CD), 0)
    return jnp.concatenate(
        [jnp.where(keep, tile[0:1], 0.0), jnp.where(keep, tile[1:2], 0.0)], axis=0
    )


def extract(full):
    group_of = iota((MODES, CD), 1) % NG
    out = jnp.zeros((MODES, CD), F32)
    for g in range(NG):
        out = jnp.where(group_of == g, full[MODES * g : MODES * (g + 1)], out)
    return out


def swap_dot(bits):
    row, lane = iota((CD, CD), 0), iota((CD, CD), 1)
    same = ((row ^ lane) & ~(3 << bits)) == 0
    row_bits, lane_bits = (row >> bits) & 3, (lane >> bits) & 3
    return jnp.concatenate(
        [
            jnp.concatenate(
                [
                    jnp.where(same & (lane_bits == i) & (row_bits == j), 1.0, 0.0).astype(BF16)
                    for j in range(4)
                ],
                axis=1,
            )
            for i in range(4)
        ],
        axis=0,
    )


def suffix(load_s, count, w):
    acc = load_s(count - 1)
    for i in range(count - 2, -1, -1):
        acc = load_s(i) + w * acc
    return acc


def pairs(load_s, load_t, count, w):
    acc = load_t(0)
    total = None
    for i in range(1, count):
        term = acc * load_s(i)
        total = term if total is None else total + term
        acc = load_t(i) + w * acc
    return total, acc


def exchange(blocks):
    bit_of = iota(blocks[0].shape, 1)
    for k in (1, 2, 4, 8):
        keep = (bit_of & k) == 0
        for i in range(NG):
            if not i & k:
                low, high = blocks[i], blocks[i | k]
                blocks[i] = jnp.where(keep, low, pltpu.roll(high, k, 1))
                blocks[i | k] = jnp.where(keep, pltpu.roll(low, CD - k, 1), high)
    return blocks


def kernel(
    x_hbm, y_hbm, res_hbm, dec_hbm, skip_hbm,
    outb, rg_ref, sg_ref,
    x, y, res_ref, dec_ref, skip_ref, xn, yn, tmp, cmc_ref, rates3, pw, pt, lags, ab, after, on, mid, swap, loc, qh, ql,
    m1, m2, m3, gz, gq,
    load_sem, send_sem, recv_sem,
):
    me = lax.axis_index("seq")
    half = lax.axis_index("chan")
    q = lax.rem(me, NQ)
    z = lax.rem(me // NQ, NZ)
    yy = me // (NQ * NZ)

    def at(y_i, z_i, q_i, h_i):
        return {"seq": (y_i * NZ + z_i) * NQ + q_i, "chan": h_i}

    quad_peers = [(k, at(yy, z, lax.rem(q + NQ - k, NQ), half)) for k in (2, 3, 1)]
    z_peers = [(k, at(yy, lax.rem(z + NZ - k, NZ), q, half)) for k in (4, 3, 5, 2, 6, 1, 7)]
    y_peers = [(k, at(lax.rem(yy + NY - k, NY), z, q, half)) for k in (2, 1, 3)]
    near = lax.rem(q + 2, NQ)
    o_peers = [(NY + k, at(lax.rem(yy + NY - k, NY), z, near, 1 - half)) for k in (2, 1, 3, 0)]

    load_y = pltpu.make_async_copy(y_hbm, y, load_sem.at[0])
    load_x = pltpu.make_async_copy(x_hbm, x, load_sem.at[1])
    load_r = pltpu.make_async_copy(res_hbm, res_ref, load_sem.at[2])
    load_d = pltpu.make_async_copy(dec_hbm, dec_ref, load_sem.at[3])
    load_k = pltpu.make_async_copy(skip_hbm, skip_ref, load_sem.at[4])
    load_d.start()
    load_y.start()
    load_x.start()
    barrier = pltpu.get_barrier_semaphore()
    everyone = z_peers + o_peers + y_peers + quad_peers
    for _, peer in everyone:
        pl.semaphore_signal(barrier, inc=1, device_id=peer, device_id_type=MESH)

    load_r.start()
    load_k.start()
    sent = []

    def send(buf, peers, sem, rows):
        for slot, peer in peers:
            pltpu.make_async_remote_copy(
                src_ref=buf.at[0, 0:rows],
                dst_ref=buf.at[slot, 0:rows],
                send_sem=send_sem.at[sem],
                recv_sem=recv_sem.at[sem],
                device_id=peer,
                device_id_type=MESH,
            ).start()
        slots = [slot for slot, _ in peers]
        area = buf.at[min(slots) : max(slots) + 1, 0:rows]
        sent.append(pltpu.make_async_copy(area, area, send_sem.at[sem]))
        return pltpu.make_async_copy(area, area, recv_sem.at[sem])

    def arrive(copies):
        copies.wait()

    swap[0] = swap_dot(0)
    swap[1] = swap_dot(2)
    load_d.wait()
    rates = dec_ref[...]
    tmp[...] = jnp.zeros_like(tmp)
    for k in range(CD // NG):
        tmp[NG * k : NG * (k + 1), 0:MODES] = rates
    rmc = jnp.transpose(tmp[...])[:MODES]
    for k in range(3):
        rates3[:, MODES * k : MODES * (k + 1)] = rates
    ahead = iota((MODES, BL), 1).astype(F32)
    behind = BL - ahead
    for g in range(NG):
        column = jnp.broadcast_to(rmc[:, g : g + 1], (MODES, BL))
        pw[MODES * g : MODES * (g + 1), :] = jnp.exp(-(column * ahead))
        pt[MODES * g : MODES * (g + 1), :] = jnp.exp(-(column * behind))

    def regroup(src, dst, step):
        for r in range(0, BL, step):
            for g, piece in enumerate(exchange([src[b * BL + r : b * BL + r + step, :] for b in range(NB)])):
                dst[g, r : r + step, :] = piece

    block_decay = jnp.exp(-(float(BL) * rmc))
    half_decay = jnp.exp(-(float(TOK // 2) * rmc))

    row_c, lane_c = iota((BL, BL), 0), iota((BL, BL), 1)
    flip = jnp.where(lane_c + row_c == BL - 1, 1.0, 0.0).astype(BF16)

    def block_states(ref, powers, flipped=None):
        hi, lo = split(powers[...])
        rates_side = jnp.concatenate([hi, lo], axis=1)
        if flipped is not None:
            flip_side = jnp.concatenate([flip, jnp.zeros_like(flip)], axis=1)
            rates_side = jnp.concatenate([rates_side, flip_side], axis=0)
        states = []
        for b in range(0, NB, 2):
            two = jnp.concatenate(
                [ref[b * BL : (b + 1) * BL, :], ref[(b + 1) * BL : (b + 2) * BL, :]], axis=1
            )
            full = nn(rates_side, jnp.concatenate([two, two], axis=0))
            states += [extract(full[:, :CD]), extract(full[:, CD:])]
            if flipped is not None:
                j, i = b // 4, b % 4
                flipped[BL * j : BL * (j + 1), CD * i : CD * (i + 2)] = full[NG * MODES :].astype(BF16)
        return states

    load_y.wait()
    run = jnp.zeros((MODES, CD), F32)
    behind_block = [None] * NB
    states = block_states(y, pw)
    for b in range(NB - 1, -1, -1):
        behind_block[b] = run
        ab[b] = run
        run = states[b] + block_decay * run
    m1[0, 0:16] = run
    load_x.wait()
    states = block_states(x, pt, mid)
    run = states[0]
    cross = run * behind_block[0]
    for b in range(1, NB):
        cross = cross + states[b] * behind_block[b]
        run = states[b] + block_decay * run
    m1[0, 16:32] = run

    part = nn(mid[...], swap[0]).astype(BF16)
    for i in range(4):
        for j in range(4):
            mid[BL * i : BL * (i + 1), CD * j : CD * (j + 1)] = part[BL * j : BL * (j + 1), CD * i : CD * (i + 1)]
    part = nn(mid[...], swap[1]).astype(BF16)
    for i in range(4):
        for j in range(4):
            xn[4 * j + i] = part[BL * i : BL * (i + 1), CD * j : CD * (j + 1)]
    regroup(y, yn, 32)

    pl.semaphore_wait(barrier, len(everyone))
    c_m1 = send(m1, quad_peers, 0, 32)
    load_r.wait()
    load_k.wait()

    for g in range(NG):
        gram = nt(xn[g], yn[g])
        gram = pltpu.roll(gram, 1, 1, stride=1, stride_axis=0)
        lags[g : g + 1, :] = jnp.sum(jnp.where(lane_c <= row_c, gram, 0.0), axis=0, keepdims=True)

    h = cross
    for g in range(NG):
        terms = pw[MODES * g : MODES * (g + 1), :] * lags[g : g + 1, :]
        column = jnp.sum(terms, axis=1, keepdims=True)
        h = h + jnp.where(iota((MODES, CD), 1) == g, column, 0.0)
    skip_sum = jnp.zeros((BL, CD), F32)
    for b in range(NB):
        rows = slice(b * BL, (b + 1) * BL)
        skip_sum = skip_sum + x[rows, :].astype(F32) * y[rows, :].astype(F32)
    skip_sum = jnp.sum(skip_sum, axis=0, keepdims=True)
    gz[0] = pack(h) + jnp.where(iota((8, CD), 0) == 2, skip_sum, 0.0)
    c_gz = send(gz, z_peers, 1, 8)

    dev = jnp.exp(-(float(TOK) * rmc))
    quad = jnp.exp(-(float(TOK * NQ) * rmc))
    slab = jnp.exp(-(float(TOK * NQ * NZ) * rmc))
    arrive(c_m1)
    load1 = lambda lo: lambda i: m1[lax.rem(i - q + NQ, NQ), lo : lo + 16]
    m2[0, 0:16] = suffix(load1(0), NQ, dev)
    p1, tq = pairs(load1(0), load1(16), NQ, dev)
    m2[0, 16:32] = tq
    m2[0, 32:40] = pack(p1)
    c_m2 = send(m2, z_peers, 2, 34)

    twice = 2.0 * rates
    series = twice * (1.0 - twice / 2 * (1.0 - twice / 3 * (1.0 - twice / 4 * (
        1.0 - twice / 5 * (1.0 - twice / 6 * (1.0 - twice / 7 * (1.0 - twice / 8)))))))
    norm = jnp.sqrt(jnp.where(twice < 0.25, series, 1.0 - jnp.exp(-twice)))
    coef = res_ref[...] * norm
    for k in range(CD // NG):
        tmp[NG * k : NG * (k + 1), 0:MODES] = coef
    cmc_ref[...] = jnp.transpose(tmp[...])[:MODES]

    third = iota((BL, 3 * MODES), 1) // MODES
    left = (BL - iota((BL, 3 * MODES), 0)).astype(F32)

    def local_one(g):
        gs = slice(MODES * g, MODES * (g + 1))
        yq = yn[g]
        column = jnp.broadcast_to(cmc_ref[:, g : g + 1], (MODES, CD))
        taps = jnp.sum(column * pw[gs, :], axis=0, keepdims=True)
        toep = pltpu.roll(jnp.broadcast_to(taps, (BL, BL)), 0, 1, stride=1, stride_axis=0)
        th, tl = split(jnp.where(lane_c >= row_c, toep, 0.0))
        ah, al = split(column * after[gs, :])
        reach = jnp.exp(-(left * rates3[g : g + 1, :]))
        rh = reach.astype(BF16).astype(F32)
        reach = jnp.where(third == 1, reach - rh, rh).astype(BF16)
        on[g] = nn(
            jnp.concatenate([th, tl], axis=1), jnp.concatenate([yq, yq], axis=0)
        ) + nn(reach, jnp.concatenate([ah, ah, al], axis=0))

    for g, piece in enumerate(exchange([ab[b] for b in range(NB)])):
        after[MODES * g : MODES * (g + 1), :] = piece
    for g in range(NG):
        local_one(g)

    skip_row = skip_ref[...].reshape(1, CD)
    for r in range(0, BL, 16):
        for b, piece in enumerate(exchange([on[g, r : r + 16, :] for g in range(NG)])):
            rows = slice(b * BL + r, b * BL + r + 16)
            loc[rows, :] = piece + skip_row * y[rows, :].astype(F32)

    def add_up(buf, count):
        total = buf[0]
        for k in range(1, count):
            total = total + buf[k]
        return total

    arrive(c_gz)
    gq[0] = add_up(gz, NZ)
    c_gq = send(gq, quad_peers, 3, 8)

    hl = TOK // 2
    column = jnp.concatenate(
        [jnp.broadcast_to(rmc[:, g : g + 1], (MODES, CD)) for g in range(NG)], axis=0
    )
    rowr = jnp.transpose(column)[0:1]
    for b in range(hl // BL):
        rows = slice(b * BL, (b + 1) * BL)
        away = (hl - b * BL - iota((BL, NG * MODES), 0)).astype(F32)
        qh[rows, :], ql[rows, :] = split(jnp.exp(-(away * rowr)))

    arrive(c_gq)
    lag_part = add_up(gq, NQ)
    arrive(c_m2)
    load2 = lambda lo: lambda i: m2[lax.rem(i - z + NZ, NZ), lo : lo + 16]
    m3[0, 0:16] = suffix(load2(0), NZ, quad)
    p2, ty = pairs(load2(0), load2(16), NZ, quad)
    m3[0, 16:32] = ty
    level = lag_part[0:2] + pack(p2)[0:2]
    for k in range(NZ):
        level = level + m2[k, 32:34]
    m3[0, 32:34] = level
    m3[0, 34:35] = lag_part[2:3]
    c_o3 = send(m3, o_peers, 4, 35)
    c_m3 = send(m3, y_peers, 5, 35)

    arrive(c_m3)
    one = jnp.ones((MODES, CD), F32)
    zero = jnp.zeros((MODES, CD), F32)
    inc_y, w = zero, one
    for k in range(1, NY):
        inc_y = inc_y + jnp.where(yy + k < NY, w, zero) * m3[k, 0:16]
        w = w * slab
    inc_z, w = zero, one
    for k in range(1, NZ):
        inc_z = inc_z + jnp.where(z + k < NZ, w, zero) * m2[k, 0:16]
        w = w * quad
    inc_q, w = zero, one
    for k in range(1, NQ):
        inc_q = inc_q + jnp.where(q + k < NQ, w, zero) * m1[k, 0:16]
        w = w * dev
    to_slab = jnp.exp(-(((NZ - 1 - z) * (TOK * NQ)).astype(F32) * rmc))
    to_quad = jnp.exp(-(((NQ - 1 - q) * TOK).astype(F32) * rmc))
    inc = inc_q + to_quad * (inc_z + to_slab * inc_y)

    late = cmc_ref[...] * inc
    early = late * half_decay
    group_of = iota((MODES, CD), 1) % NG

    def spread(v):
        return jnp.concatenate([jnp.where(group_of == g, v, 0.0) for g in range(NG)], axis=0)

    def both(v, u):
        return jnp.concatenate([spread(v), spread(u)], axis=1).astype(BF16)

    eh = early.astype(BF16).astype(F32)
    lh = late.astype(BF16).astype(F32)
    a_hi = both(eh, lh)
    a_lo = both(early - eh, late - lh)
    arrived = jnp.concatenate([a_hi, a_lo, a_hi], axis=0)
    step = 2 * BL
    for r in range(0, hl, step):
        rows, rows2 = slice(r, r + step), slice(hl + r, hl + r + step)
        hi, lo = qh[rows, :], ql[rows, :]
        add = nn(jnp.concatenate([hi, hi, lo], axis=1), arrived)
        outb[rows, :] = (loc[rows, :] + add[:, :CD]).astype(BF16)
        outb[rows2, :] = (loc[rows2, :] + add[:, CD:]).astype(BF16)

    for copy in sent[:-2]:
        copy.wait()
    total_len = TOK * NQ * NZ * NY
    load3 = lambda lo, base: lambda i: m3[base + lax.rem(i - yy + NY, NY), lo : lo + 16]
    p3, _ = pairs(load3(0, 0), load3(16, 0), NY, slab)
    base = m3[0, 32:35] + m3[1, 32:35] + m3[2, 32:35] + m3[3, 32:35]
    sg_ref[...] = (base[2:3] * (1.0 / math.sqrt(total_len))).reshape(CD)
    arrive(c_o3)
    p4, _ = pairs(load3(0, NY), load3(16, NY), NY, slab)
    base = base + m3[4, 32:35] + m3[5, 32:35] + m3[6, 32:35] + m3[7, 32:35]
    grads = fold(unpack(base) + p3 + p4)
    tmp[...] = jnp.zeros_like(tmp)
    tmp[0:MODES, :] = grads
    turned = jnp.transpose(tmp[...])[0:NG, 0:MODES]
    rg_ref[...] = turned * norm * (1.0 / math.sqrt(GROUP * total_len))

    for copy in sent[-2:]:
        copy.wait()


def deliver(a, b, c, to_a, to_b, to_c, sems):
    copies = [
        pltpu.make_async_copy(src, dst, sems.at[i])
        for i, (src, dst) in enumerate(((a, to_a), (b, to_b), (c, to_c)))
    ]
    for copy in copies:
        copy.start()
    for copy in copies:
        copy.wait()


def shards(inputs, cotangent, residues, decay_rates, skip_weight):
    vmem = pl.BlockSpec(memory_space=pltpu.VMEM)
    hbm = pl.BlockSpec(memory_space=pltpu.HBM)
    near = pl.pallas_call(
        kernel,
        out_shape=(
            pltpu.VMEM((TOK, CD), BF16),
            pltpu.VMEM((NG, MODES), F32),
            pltpu.VMEM((CD,), F32),
        ),
        in_specs=[hbm] * 5,
        out_specs=(vmem, vmem, vmem),
        scratch_shapes=[
            pltpu.VMEM((TOK, CD), BF16),
            pltpu.VMEM((TOK, CD), BF16),
            pltpu.VMEM((NG, MODES), F32),
            pltpu.VMEM((NG, MODES), F32),
            pltpu.VMEM((CD,), F32),
            pltpu.VMEM((NG, BL, CD), BF16),
            pltpu.VMEM((NG, BL, CD), BF16),
            pltpu.VMEM((CD, CD), F32),
            pltpu.VMEM((MODES, CD), F32),
            pltpu.VMEM((NG, 3 * MODES), F32),
            pltpu.VMEM((NG * MODES, BL), F32),
            pltpu.VMEM((NG * MODES, BL), F32),
            pltpu.VMEM((NG, BL), F32),
            pltpu.VMEM((NB, MODES, CD), F32),
            pltpu.VMEM((NG * MODES, CD), F32),
            pltpu.VMEM((NG, BL, CD), F32),
            pltpu.VMEM((4 * BL, 4 * CD), BF16),
            pltpu.VMEM((2, 4 * CD, 4 * CD), BF16),
            pltpu.VMEM((TOK, CD), F32),
            pltpu.VMEM((TOK // 2, NG * MODES), BF16),
            pltpu.VMEM((TOK // 2, NG * MODES), BF16),
            pltpu.VMEM((NQ, 32, CD), F32),
            pltpu.VMEM((NZ, 40, CD), F32),
            pltpu.VMEM((2 * NY, 40, CD), F32),
            pltpu.VMEM((NZ, 8, CD), F32),
            pltpu.VMEM((NQ, 8, CD), F32),
            pltpu.SemaphoreType.DMA((5,)),
            pltpu.SemaphoreType.DMA((6,)),
            pltpu.SemaphoreType.DMA((6,)),
        ],
        compiler_params=pltpu.CompilerParams(
            collective_id=0, has_side_effects=True, vmem_limit_bytes=32 << 20
        ),
    )(*[pltpu.with_memory_space_constraint(v, pltpu.HBM) for v in (inputs, cotangent, residues, decay_rates, skip_weight)])
    return pl.pallas_call(
        deliver,
        out_shape=(
            jax.ShapeDtypeStruct((TOK, CD), BF16),
            jax.ShapeDtypeStruct((NG, MODES), F32),
            jax.ShapeDtypeStruct((CD,), F32),
        ),
        in_specs=[vmem, vmem, vmem],
        out_specs=(hbm, hbm, hbm),
        scratch_shapes=[pltpu.SemaphoreType.DMA((3,))],
    )(*[pltpu.with_memory_space_constraint(v, pltpu.VMEM) for v in near])


def solution(mesh):
    placed = (P("seq", "chan"), P("seq", "chan"), P(), P(), P("chan"))
    return jax.shard_map(
        shards,
        mesh=mesh,
        in_specs=placed,
        out_specs=(P("seq", "chan"), P(), P("chan")),
        check_vma=False,
    )
```
